256 devices in a mesh: src: 64 (over z, y, core), rhs: 4 (over x).
Axes of the slice: x: 4, y: 4, z: 8, core: 2. Of those that a mesh axis runs over, the one named last changes fastest.
Arguments:
- coefficients: bfloat16 [4096, 256, 64], P('src', 'rhs'), may hold values from -6 to 6
- pairing: int32 [8, 64, 64], P(None, 'src'), may hold values from 0 to 63, each once within a row
- level_weights: bfloat16 [8, 4096, 64, 128], P(None, 'src'), may hold values from -0.5 to 0.5
- middle_weights: bfloat16 [4096, 64, 64], P('src'), may hold values from -0.75 to 0.75
Outputs:
- target_coefficients: bfloat16 [4096, 256, 64], P('src', 'rhs')
The draws below stay inside these ranges and needn't reach their ends.
Inputs may be any that keep to these rules, and one draw needn't show every extreme that they name: Each row pairing[l, d, :] is a permutation of 0 to 63.
All inputs are finite; a program needn't handle non-finite values.
Results may differ from the reference program's by a relative error of at most 0.014.
Values may be sent and summed in bfloat16 or wider, within the bound.
A program may use at most 64 MiB of HBM per device.

```python
import jax
import jax.numpy as jnp

K = 64
B_DEV = 64
LEVELS = 8
NB = 4096
COLS = 256
N_SRC = 64


def level_of(stream_key, extent, split, least, largest):
    level = 1.0
    for dim, parts in split:
        steps = jax.random.uniform(jax.random.fold_in(jax.random.fold_in(stream_key, 6), dim), (parts,), jnp.float32, least / len(split), largest / len(split))
        level = level * jnp.repeat(jnp.exp(steps), extent[dim] // parts).reshape((-1,) + (1,) * (len(extent) - 1 - dim))
    return level


def bell_draw(rng, dims, scale, limit, split=(), held_as=jnp.bfloat16):
    values = scale * jax.random.normal(rng, dims, jnp.float32)
    if split:
        values = values * level_of(rng, dims, split, -0.22, 0.18)
    return jnp.clip(values, -limit, limit).astype(held_as)


def setup_inputs(seed: int = 0) -> dict:
    keys = jax.random.split(jax.random.key(seed), 5)
    return {
        "coefficients": bell_draw(keys[0], (NB, COLS, K), 1.0, 6.0, ((0, 64), (1, 4))),
        "pairing": jax.vmap(lambda own: jax.random.permutation(own, B_DEV))(jax.random.split(keys[1], LEVELS * N_SRC)).reshape((LEVELS, N_SRC, B_DEV)).astype(jnp.int32),
        "level_weights": bell_draw(keys[2], (LEVELS, NB, K, 2 * K), (2 * K) ** -0.5, 0.5, ((1, 64),)),
        "middle_weights": bell_draw(keys[3], (NB, K, K), K ** -0.5, 0.75, ((0, 64),)),
    }


def level_apply(state, pairing_level, weight, bit):
    total = state.shape[0]
    index = jnp.arange(total, dtype=jnp.int32)
    device = index // B_DEV
    partner_dev = jnp.bitwise_xor(device, jnp.int32(1 << bit))
    partner = partner_dev * B_DEV + pairing_level.reshape(-1).astype(jnp.int32)
    other = state[partner]
    own = jnp.einsum("gcj,gkj->gck", state.astype(jnp.float32), weight[:, :, :K].astype(jnp.float32))
    far = jnp.einsum("gcj,gkj->gck", other.astype(jnp.float32), weight[:, :, K:].astype(jnp.float32))
    return (own + far).astype(jnp.bfloat16)


def reference(coefficients, pairing, level_weights, middle_weights):
    bits = int(N_SRC).bit_length() - 1
    state = coefficients
    half = LEVELS // 2
    for level in range(half):
        state = level_apply(state, pairing[level], level_weights[level], level % bits)
    share = B_DEV // N_SRC
    moved = state.reshape(N_SRC, N_SRC, share, state.shape[1], K)
    moved = jnp.transpose(moved, (1, 0, 2, 3, 4)).reshape(state.shape)
    state = jnp.einsum("gcj,gkj->gck", moved.astype(jnp.float32), middle_weights.astype(jnp.float32)).astype(jnp.bfloat16)
    for level in range(half, LEVELS):
        state = level_apply(state, pairing[level], level_weights[level], level % bits)
    return state
```

```python
import functools

import jax
import jax.numpy as jnp
from jax import lax
from jax.experimental import pallas as pl
from jax.experimental.pallas import tpu as pltpu
from jax.sharding import PartitionSpec as P

LEVELS = 8
HALF = 4
BITS = 6
B = 64
K = 64
C = 64
Q = 2
R = C // Q // 2
PIECES = 4
PB = B // PIECES
MESH = pl.DeviceIdType.MESH


def kernel(coef, pairing, lw, mw, out, x_in, w, m, st, t1, mv, y_out,
           in_sem, w_sem, m_sem, out_sem, lvl_send, lvl_recv, z_send, z_recv, y_send, y_recv, own_sem, *rv):
    me = lax.axis_index("src")
    rhs = lax.axis_index("rhs")
    z, yc = me // 8, me % 8

    load_x = pltpu.make_async_copy(coef, x_in, in_sem)
    load_x.start()
    load_w = [pltpu.make_async_copy(lw.at[l], w.at[l], w_sem.at[l]) for l in range(LEVELS)]
    load_m = pltpu.make_async_copy(mw, m, m_sem)

    def at(s):
        return (s, rhs)

    def partner(h):
        return me + (1 << h) * (1 - 2 * ((me // (1 << h)) % 2))

    z_peers = [((z + k) % 8) * 8 + yc for k in range(1, 8)]
    y_peers = [z * 8 + (yc + k) % 8 for k in range(1, 8)]
    barrier = pltpu.get_barrier_semaphore()
    for s in z_peers + y_peers:
        pl.semaphore_signal(barrier, inc=1, device_id=at(s), device_id_type=MESH)
    for l in range(HALF):
        load_w[l].start()
    load_m.start()
    for l in range(HALF, LEVELS):
        load_w[l].start()

    def level_copy(l, q, piece):
        blocks = pl.ds(piece * PB, PB)
        src = st.at[l if l < HALF else l + 1, q, blocks]
        return pltpu.make_async_remote_copy(
            src_ref=src, dst_ref=rv[l * Q + q].at[blocks],
            send_sem=lvl_send.at[l, q, piece], recv_sem=lvl_recv.at[l, q, piece],
            device_id=at(partner(l % BITS)), device_id_type=MESH)

    def z_copy(q, k):
        return pltpu.make_async_remote_copy(
            src_ref=st.at[HALF, q, pl.ds(((z + k) % 8) * 8, 8)], dst_ref=t1.at[q, z],
            send_sem=z_send.at[q, k], recv_sem=z_recv.at[q, k],
            device_id=at(z_peers[k - 1]), device_id_type=MESH)

    def y_copy(q, k):
        return pltpu.make_async_remote_copy(
            src_ref=t1.at[q, :, (yc + k) % 8], dst_ref=mv.at[q, :, yc],
            send_sem=y_send.at[q, k], recv_sem=y_recv.at[q, k],
            device_id=at(y_peers[k - 1]), device_id_type=MESH)

    lane = lax.broadcasted_iota(jnp.int32, (K, 2 * K), 1)
    low = lane < K

    def spread(pair):
        zero = jnp.zeros_like(pair)
        turned = jnp.concatenate([pair[:, K:], pair[:, :K]], axis=1)
        top = jnp.concatenate([jnp.where(low, pair, zero), jnp.where(low, turned, zero)], axis=1)
        bottom = jnp.concatenate([jnp.where(low, zero, turned), jnp.where(low, zero, pair)], axis=1)
        return jnp.concatenate([top, bottom], axis=0)

    def times(x, weight):
        return lax.dot_general(x, weight, (((1,), (1,)), ((), ())), preferred_element_type=jnp.float32)

    def level(l, q):
        src = l if l < HALF else l + 1
        @pl.loop(0, PIECES)
        def _(piece):
            level_copy(l, q, piece).wait_recv()

        @pl.loop(0, PIECES)
        def _(piece):
            for i in range(PB):
                b = piece * PB + i
                own = st[src, q, b]
                far = rv[l * Q + q][pairing[l, 0, b]]
                acc = times(jnp.concatenate([own, far], axis=1), spread(w[l, b]))
                new = acc.astype(jnp.bfloat16)
                if l < LEVELS - 1:
                    st[src + 1, q, b] = new
                else:
                    y_out[b, pl.ds(q * 2 * R, R), :] = new[:, :K]
                    y_out[b, pl.ds(q * 2 * R + R, R), :] = new[:, K:]
            if l < LEVELS - 1 and l != HALF - 1:
                level_copy(l + 1, q, piece).start()

    load_x.wait()
    for q in range(Q):
        @pl.loop(0, PIECES)
        def _(piece):
            for i in range(PB):
                b = piece * PB + i
                st[0, q, b] = jnp.concatenate(
                    [x_in[b, q * 2 * R:q * 2 * R + R, :], x_in[b, q * 2 * R + R:(q + 1) * 2 * R, :]], axis=1)

    pl.semaphore_wait(barrier, 14)
    for q in range(Q):
        @pl.loop(0, PIECES)
        def _(piece):
            level_copy(0, q, piece).start()

    for l in range(HALF):
        load_w[l].wait()
        for q in range(Q):
            level(l, q)
            if l == HALF - 1:
                for k in (4, 3, 5, 2, 6, 1, 7):
                    z_copy(q, k).start()
                own = pltpu.make_async_copy(st.at[HALF, q, pl.ds(z * 8, 8)], t1.at[q, z], own_sem.at[0, q])
                own.start()

    load_m.wait()
    for q in range(Q):
        for k in range(1, 8):
            z_copy(q, k).wait_recv()
        pltpu.make_async_copy(st.at[HALF, q, pl.ds(z * 8, 8)], t1.at[q, z], own_sem.at[0, q]).wait()
        for k in (4, 3, 5, 2, 6, 1, 7):
            y_copy(q, k).start()
        pltpu.make_async_copy(t1.at[q, :, yc], mv.at[q, :, yc], own_sem.at[1, q]).start()

    for q in range(Q):
        for k in range(1, 8):
            y_copy(q, k).wait_recv()
        pltpu.make_async_copy(t1.at[q, :, yc], mv.at[q, :, yc], own_sem.at[1, q]).wait()

        @pl.loop(0, PIECES)
        def _(piece):
            for i in range(PB):
                b = piece * PB + i
                mb = m[b]
                zero = jnp.zeros_like(mb)
                weight = jnp.concatenate(
                    [jnp.concatenate([mb, zero], axis=1), jnp.concatenate([zero, mb], axis=1)], axis=0)
                st[HALF + 1, q, b] = times(mv[q, piece * (PB // 8) + i // 8, i % 8], weight).astype(jnp.bfloat16)
            level_copy(HALF, q, piece).start()

    for l in range(HALF, LEVELS):
        load_w[l].wait()
        for q in range(Q):
            level(l, q)

    store = pltpu.make_async_copy(y_out, out, out_sem)
    store.start()
    for q in range(Q):
        for l in range(LEVELS):
            @pl.loop(0, PIECES)
            def _(piece):
                level_copy(l, q, piece).wait_send()
        for k in range(1, 8):
            z_copy(q, k).wait_send()
            y_copy(q, k).wait_send()
    store.wait()


def body(coefficients, pairing, level_weights, middle_weights):
    bf16 = jnp.bfloat16
    dma = pltpu.SemaphoreType.DMA
    any_space = pl.BlockSpec(memory_space=pl.ANY)
    return pl.pallas_call(
        kernel,
        out_shape=jax.ShapeDtypeStruct((B, C, K), bf16),
        in_specs=[any_space, pl.BlockSpec(memory_space=pltpu.SMEM), any_space, any_space],
        out_specs=any_space,
        scratch_shapes=[
            pltpu.VMEM((B, C, K), bf16),
            pltpu.VMEM((LEVELS, B, K, 2 * K), bf16),
            pltpu.VMEM((B, K, K), bf16),
            pltpu.VMEM((LEVELS + 1, Q, B, R, 2 * K), bf16),
            pltpu.VMEM((Q, 8, 8, R, 2 * K), bf16),
            pltpu.VMEM((Q, 8, 8, R, 2 * K), bf16),
            pltpu.VMEM((B, C, K), bf16),
            dma, dma((LEVELS,)), dma, dma,
            dma((LEVELS, Q, PIECES)), dma((LEVELS, Q, PIECES)),
            dma((Q, 8)), dma((Q, 8)), dma((Q, 8)), dma((Q, 8)), dma((2, Q)),
        ] + [pltpu.VMEM((B, R, 2 * K), bf16)] * (LEVELS * Q),
        compiler_params=pltpu.CompilerParams(
            collective_id=0, has_side_effects=True, vmem_limit_bytes=48 * 1024 * 1024),
    )(coefficients, pairing, level_weights, middle_weights)


def solution(mesh):
    placed = (
        P("src", "rhs", None),
        P(None, "src", None),
        P(None, "src", None, None),
        P("src", None, None),
    )
    return jax.shard_map(
        body, mesh=mesh, in_specs=placed, out_specs=P("src", "rhs", None), check_vma=False
    )
```

```python
import jax
import jax.numpy as jnp
from jax import lax
from jax.experimental import pallas as pl
from jax.experimental.pallas import tpu as pltpu
from jax.sharding import PartitionSpec as P

LEVELS = 8
N = 64
B = 64
K = 64
C = 64
Q = 2
H = C // Q // 2
PIECES = 4
PB = B // PIECES
PP = PB // 2
X = 4
MESH = pl.DeviceIdType.MESH
SKEW = 0


def kernel(coef, pairing, pairing_any, lw, mw, out,
           x_in, w, m, w_x, m_x, m_send, pair_v, pair_s, y_out,
           st0, st1, st2, st3, moved_from, st6, st7,
           in_sem, w_sem, m_sem, out_sem, pair_sem, own_sem,
           lvl_send, lvl_recv, a_send, a_recv, e_send, e_recv, wz_send, wz_recv, wx_send, wx_recv,
           *per_chunk):
    me = lax.axis_index("src")
    rhs = lax.axis_index("rhs")
    z = me // 8
    zb1 = (z // 2) % 2
    n_lists = 9
    r0, r1, r2, r3, r6, r7, mv, t4, far5 = [per_chunk[i * Q:(i + 1) * Q] for i in range(n_lists)]
    own5, oth5, ret5 = [per_chunk[(n_lists + i) * Q:(n_lists + i + 1) * Q] for i in range(3)]
    recv_of = {0: r0, 1: r1, 2: r2, 3: r3, 6: r6, 7: r7}
    state_of = {0: st0, 1: st1, 2: st2, 3: st3, 6: st6, 7: st7}

    load_x = pltpu.make_async_copy(coef, x_in, in_sem)
    load_x.start()
    load_w = [pltpu.make_async_copy(lw.at[l], w.at[l], w_sem.at[l]) for l in range(LEVELS)]
    load_m = pltpu.make_async_copy(mw, m, m_sem)
    load_m.start()

    def flipped(s, h):
        return s + (1 << h) * (1 - 2 * ((s // (1 << h)) % 2))

    far_x = [(rhs + k) % X for k in range(1, X)]
    barrier = pltpu.get_barrier_semaphore()

    @pl.loop(1, N)
    def _(k):
        pl.semaphore_signal(barrier, inc=1, device_id=((me + k) % N, rhs), device_id_type=MESH)

    for x in far_x:
        pl.semaphore_signal(barrier, inc=1, device_id=(me, x), device_id_type=MESH)
    for l in range(LEVELS):
        load_w[l].start()

    def remote(src, dst, send, recv, dev, x=None):
        return pltpu.make_async_remote_copy(
            src_ref=src, dst_ref=dst, send_sem=send, recv_sem=recv,
            device_id=(dev, rhs if x is None else x), device_id_type=MESH)

    def level_copy(l, q, piece):
        blocks = pl.ds(piece * PB, PB)
        return remote(state_of[l].at[q, blocks], recv_of[l][q].at[blocks],
                      lvl_send.at[l, q, piece], lvl_recv.at[l, q, piece], flipped(me, l % 6))

    def a2a_copy(q, e):
        return remote(moved_from.at[q, e], mv[q].at[me], a_send.at[q], a_recv.at[q], e)

    def a2a_all(q):
        return remote(moved_from.at[q, pl.ds(0, N - 1)], mv[q].at[pl.ds(0, N - 1)],
                      a_send.at[q], a_recv.at[q], flipped(me, 0))

    def a2a_own(q):
        return pltpu.make_async_copy(moved_from.at[q, me], mv[q].at[me], own_sem.at[q])

    def merged_copies(q, piece):
        pairs = pl.ds(piece * PP, PP)
        e16, e32 = flipped(me, 4), flipped(me, 5)
        e48 = flipped(e16, 5)
        return [
            remote(own5[q].at[pairs], far5[q].at[0, pairs], e_send.at[0, q, piece], e_recv.at[0, q, piece], e32),
            remote(oth5[q].at[pairs], far5[q].at[1, pairs], e_send.at[1, q, piece], e_recv.at[1, q, piece], e48),
            remote(oth5[q].at[pairs], ret5[q].at[pairs], e_send.at[2, q, piece], e_recv.at[2, q, piece], e16),
        ]

    quarter_w, quarter_m = pl.ds(rhs * (B // X), B // X), pl.ds(rhs * (B // 2 // X), B // 2 // X)

    def weight_z():
        e16 = flipped(me, 4)
        return [
            remote(m_send.at[quarter_m], m_x.at[quarter_m], wz_send.at[0], wz_recv.at[0], e16),
            remote(lw.at[4, quarter_w], w_x.at[quarter_w], wz_send.at[1], wz_recv.at[1], e16),
            remote(pairing_any, pair_v, wz_send.at[2], wz_recv.at[2], e16),
        ]

    def weight_x(which):
        ref, quarter = ((m_x, quarter_m), (w_x, quarter_w))[which]
        return [remote(ref.at[quarter], ref.at[quarter], wx_send.at[which, k], wx_recv.at[which, k], me, far_x[k])
                for k in range(X - 1)]

    low_w = lax.broadcasted_iota(jnp.int32, (K, 2 * K), 1) < K
    low_t = lax.broadcasted_iota(jnp.int32, (H, 2 * K), 1) < K

    def turned(x):
        return jnp.concatenate([x[:, K:], x[:, :K]], axis=1)

    def lo(x):
        return jnp.where(low_w, x, jnp.zeros_like(x))

    def hi(x):
        return jnp.where(low_w, jnp.zeros_like(x), x)

    def first_rows(pair):
        return jnp.concatenate([lo(pair), hi(pair)], axis=1)

    def second_rows(pair):
        back = turned(pair)
        return jnp.concatenate([hi(back), lo(back)], axis=1)

    def times(x, *rows):
        weight = jnp.concatenate(rows, axis=0)
        return lax.dot_general(x, weight, (((1,), (1,)), ((), ())), preferred_element_type=jnp.float32)

    def beside(own, far):
        return jnp.concatenate([own, far], axis=1)

    def plain(l, q, b, swap=False):
        own = state_of[l][q, b]
        far = turned(recv_of[l][q][pairing[l, 0, b]])
        rows = first_rows(w[l, b]), second_rows(w[l, b])
        return times(beside(own, far), *(rows[::-1] if swap else rows))

    def bf16(x):
        return x.astype(jnp.bfloat16)

    def begin(q):
        @pl.loop(0, PIECES)
        def _(piece):
            for i in range(PB):
                b = piece * PB + i
                st0[q, b] = beside(x_in[b, 2 * q * H:(2 * q + 1) * H, :], x_in[b, (2 * q + 1) * H:(2 * q + 2) * H, :])

    def send_level(l, q):
        @pl.loop(0, PIECES)
        def _(piece):
            level_copy(l, q, piece).start()

    def wait_level(l, q):
        @pl.loop(0, PIECES)
        def _(piece):
            level_copy(l, q, piece).wait_recv()

    def plain_level(l, q):
        wait_level(l, q)

        @pl.loop(0, PIECES)
        def _(piece):
            for i in range(PB):
                b = piece * PB + i
                new = bf16(plain(l, q, b))
                if l < LEVELS - 1:
                    state_of[l + 1][q, b] = new
                else:
                    at = pl.multiple_of(2 * q * H + zb1 * H, H)
                    y_out[b, pl.ds(at, H), :] = new[:, :K]
                    at = pl.multiple_of((2 * q + 1) * H - zb1 * H, H)
                    y_out[b, pl.ds(at, H), :] = new[:, K:]
            if l < LEVELS - 1:
                level_copy(l + 1, q, piece).start()

    def last_source_level(q):
        wait_level(3, q)

        @pl.loop(0, PIECES)
        def _(i):
            piece = (i + z // 2) % PIECES
            base = (piece // 2) * (N // 2) + (piece % 2) * PP
            for j in range(PP):
                b = base + j
                one = plain(3, q, b)
                two = plain(3, q, b + 16, swap=True)
                moved_from[q, b] = bf16(jnp.where(low_t, one, two))
                moved_from[q, b + 16] = bf16(jnp.where(low_t, two, one))

            @pl.loop(0, PP)
            def _(j):
                for e in (base + j, base + j + 16):
                    @pl.when(e != me)
                    def _():
                        a2a_copy(q, e).start()

                    @pl.when(e == me)
                    def _():
                        a2a_own(q).start()

    def middle_and_level4(q):
        a2a_all(q).wait_recv()
        a2a_own(q).wait()

        @pl.loop(0, PIECES)
        def _(piece):
            for j in range(PP):
                d = piece * PP + j
                theirs = m_x[d]
                zero = jnp.zeros((K, K), jnp.bfloat16)
                for s, other in ((d, hi(theirs)), (d + B // 2, hi(turned(theirs)))):
                    t4[q][s] = bf16(times(mv[q][s], beside(m[s], zero), other))

        @pl.loop(0, PIECES)
        def _(piece):
            for j in range(PP):
                i = piece * PP + j
                new = []
                for b, swap in ((i, False), (i + B // 2, True)):
                    far = jnp.where(low_t, t4[q][pair_s[4, 0, b]], t4[q][pairing[4, 0, b]])
                    rows = first_rows(w[4, b]), second_rows(w_x[b])
                    new.append(times(beside(t4[q][b], far), *(rows[::-1] if swap else rows)))
                own5[q][i] = bf16(jnp.where(low_t, new[0], new[1]))
                oth5[q][i] = bf16(jnp.where(low_t, new[1], new[0]))
            for copy in merged_copies(q, piece):
                copy.start()

    def level5(q):
        @pl.loop(0, PIECES)
        def _(piece):
            for copy in merged_copies(q, piece):
                copy.wait_recv()

        @pl.loop(0, PIECES)
        def _(piece):
            for j in range(PP):
                i = piece * PP + j
                for b, upper in ((i, 0), (i + B // 2, 1)):
                    mine, back = own5[q][i], ret5[q][i]
                    own = jnp.where(low_t, back, mine) if upper else jnp.where(low_t, mine, back)
                    p = pairing[5, 0, b]
                    at, half = p % (B // 2), p // (B // 2)
                    far = jnp.where(low_t, far5[q][half, at], far5[q][1 - half, at])
                    far = jnp.where(half == upper, turned(far), far)
                    rows = first_rows(w[5, b]), second_rows(w[5, b])
                    st6[q, b] = bf16(times(beside(own, far), *(rows[::-1] if upper else rows)))

        send_level(6, q)

    waited = set()

    def need(*names):
        for name in names:
            if name not in waited:
                waited.add(name)
                if name == "m":
                    load_m.wait()
                elif name == "x":
                    for which in range(2):
                        for copy in weight_x(which):
                            copy.wait_recv()
                    to_smem = pltpu.make_async_copy(pair_v, pair_s, pair_sem)
                    to_smem.start()
                    to_smem.wait()
                else:
                    load_w[name].wait()

    def forward():
        for which, crossing in enumerate(weight_z()):
            crossing.wait_recv()
            if which < 2:
                for copy in weight_x(which):
                    copy.start()

    def store(q):
        rows = pl.ds(2 * q * H, 2 * H)
        return pltpu.make_async_copy(y_out.at[:, rows], out.at[:, rows], out_sem.at[q])

    def task(t, q):
        if t < 3:
            need(t)
            plain_level(t, q)
        elif t == 3:
            need(3)
            last_source_level(q)
        elif t == 4:
            need("m", "x", 4)
            middle_and_level4(q)
        elif t == 5:
            need(5)
            level5(q)
        else:
            need(t)
            plain_level(t, q)
            if t == 7:
                store(q).start()
        if t == 1 and q == Q - 1:
            forward()

    load_x.wait()
    begin(0)
    pl.semaphore_wait(barrier, N - 1 + X - 1)
    send_level(0, 0)
    for q in range(1, Q):
        begin(q)
        send_level(0, q)
    need("m")
    for d in range(B // 2):
        m_send[d] = beside(m[d + B // 2], m[d])
    for copy in weight_z():
        copy.start()
    for _, q, t in sorted((t + SKEW * q, q, t) for q in range(Q) for t in range(8)):
        task(t, q)

    for copy in weight_z() + weight_x(0) + weight_x(1):
        copy.wait_send()
    for q in range(Q):
        @pl.loop(0, PIECES)
        def _(piece):
            for l in (0, 1, 2, 3, 6, 7):
                level_copy(l, q, piece).wait_send()
            for copy in merged_copies(q, piece):
                copy.wait_send()
        a2a_all(q).wait_send()
    for q in range(Q):
        store(q).wait()


def body(coefficients, pairing, level_weights, middle_weights):
    bf16 = jnp.bfloat16
    dma = pltpu.SemaphoreType.DMA
    any_space = pl.BlockSpec(memory_space=pl.ANY)
    tiles = pltpu.VMEM((Q, B, H, 2 * K), bf16)
    full = pltpu.VMEM((B, H, 2 * K), bf16)
    half = pltpu.VMEM((B // 2, H, 2 * K), bf16)
    both = pltpu.VMEM((2, B // 2, H, 2 * K), bf16)
    return pl.pallas_call(
        kernel,
        out_shape=jax.ShapeDtypeStruct((B, C, K), bf16),
        in_specs=[any_space, pl.BlockSpec(memory_space=pltpu.SMEM), any_space, any_space, any_space],
        out_specs=any_space,
        scratch_shapes=[
            pltpu.VMEM((B, C, K), bf16),
            pltpu.VMEM((LEVELS, B, K, 2 * K), bf16),
            pltpu.VMEM((B, K, K), bf16),
            pltpu.VMEM((B, K, 2 * K), bf16),
            pltpu.VMEM((B // 2, K, 2 * K), bf16),
            pltpu.VMEM((B // 2, K, 2 * K), bf16),
            pltpu.VMEM((LEVELS, 1, B), jnp.int32),
            pltpu.SMEM((LEVELS, 1, B), jnp.int32),
            pltpu.VMEM((B, C, K), bf16),
        ] + [tiles] * 7 + [
            dma, dma((LEVELS,)), dma, dma((Q,)), dma, dma((Q,)),
            dma((LEVELS, Q, PIECES)), dma((LEVELS, Q, PIECES)), dma((Q,)), dma((Q,)),
            dma((3, Q, PIECES)), dma((3, Q, PIECES)), dma((3,)), dma((3,)), dma((2, X - 1)), dma((2, X - 1)),
        ] + [full] * (8 * Q) + [both] * Q + [half] * (3 * Q),
        compiler_params=pltpu.CompilerParams(
            collective_id=0, has_side_effects=True, vmem_limit_bytes=60 * 1024 * 1024),
    )(coefficients, pairing, pairing, level_weights, middle_weights)


def solution(mesh):
    placed = (
        P("src", "rhs", None),
        P(None, "src", None),
        P(None, "src", None, None),
        P("src", None, None),
    )
    return jax.shard_map(
        body, mesh=mesh, in_specs=placed, out_specs=P("src", "rhs", None), check_vma=False
    )
```

```python
import jax
import jax.numpy as jnp
from jax import lax
from jax.experimental import pallas as pl
from jax.experimental.pallas import tpu as pltpu
from jax.sharding import PartitionSpec as P

LEVELS = 8
N = 64
B = 64
K = 64
C = 64
Q = 4
H = C // Q
T = B // 2
PIECES = 2
PT = T // PIECES
X = 4
MESH = pl.DeviceIdType.MESH


def kernel(coef, pairing, pairing_any, lw, mw, out,
           x_in, w, m, w_x, m_x, m_send, pair_v, pair_s, y_out,
           in_sem, w_sem, m_sem, out_sem, pair_sem, own_sem,
           lvl_send, lvl_recv, a_send, a_recv, e_send, e_recv, wz_send, wz_recv, wx_send, wx_recv,
           *per_chunk):
    me = lax.axis_index("src")
    rhs = lax.axis_index("rhs")
    z = me // 8
    zb1 = (z // 2) % 2

    lists = [per_chunk[i * Q:(i + 1) * Q] for i in range(len(per_chunk) // Q)]
    s0, s1, s2, s3, s4, s5, s6, s7, r0, r1, r2, r3, r5, r6, r7, other5, moved, t4 = lists
    state, far_of = (s0, s1, s2, s3, s4, s5, s6, s7), (r0, r1, r2, r3, None, r5, r6, r7)

    load_x = pltpu.make_async_copy(coef, x_in, in_sem)
    load_x.start()
    load_w = [pltpu.make_async_copy(lw.at[l], w.at[l], w_sem.at[l]) for l in range(LEVELS)]
    load_m = pltpu.make_async_copy(mw, m, m_sem)
    load_m.start()

    def flipped(s, h):
        return s + (1 << h) * (1 - 2 * ((s // (1 << h)) % 2))

    e16, e32 = flipped(me, 4), flipped(me, 5)
    e48 = flipped(e16, 5)
    far_x = [(rhs + k) % X for k in range(1, X)]
    barrier = pltpu.get_barrier_semaphore()

    @pl.loop(1, N)
    def _(k):
        pl.semaphore_signal(barrier, inc=1, device_id=((me + k) % N, rhs), device_id_type=MESH)

    for x in far_x:
        pl.semaphore_signal(barrier, inc=1, device_id=(me, x), device_id_type=MESH)
    for l in range(LEVELS):
        load_w[l].start()

    def remote(src, dst, send, recv, dev, x=None):
        return pltpu.make_async_remote_copy(
            src_ref=src, dst_ref=dst, send_sem=send, recv_sem=recv,
            device_id=(dev, rhs if x is None else x), device_id_type=MESH)

    def level_copy(l, q, piece):
        tiles = pl.ds(piece * PT, PT)
        return remote(state[l][q].at[tiles], far_of[l][q].at[tiles],
                      lvl_send.at[l, q, piece], lvl_recv.at[l, q, piece], flipped(me, l % 6))

    def a2a_copy(q, i, e):
        return remote(s4[q].at[i], moved[q].at[me], a_send.at[q], a_recv.at[q], e)

    def a2a_own(q, i):
        return pltpu.make_async_copy(s4[q].at[i], moved[q].at[me], own_sem.at[q])

    def a2a_recv_all(q):
        return remote(moved[q].at[pl.ds(0, N - 1)], moved[q].at[pl.ds(0, N - 1)], a_send.at[q], a_recv.at[q], e16)

    def a2a_send_all(q, n):
        return remote(s4[q].at[pl.ds(0, n)], s4[q].at[pl.ds(0, n)], a_send.at[q], a_recv.at[q], e16)

    def far5_copy(q, piece):
        tiles = pl.ds(piece * PT, PT)
        return remote(s5[q].at[tiles], r5[q].at[tiles], e_send.at[0, q, piece], e_recv.at[0, q, piece], e32)

    def other_copies(q, piece):
        tiles = pl.ds(piece * PT, PT)
        src = other5[q].at[tiles]
        return (remote(src, r5[q].at[tiles], e_send.at[1, q, piece], e_recv.at[0, q, piece], e48),
                remote(src, s5[q].at[tiles], e_send.at[2, q, piece], e_recv.at[1, q, piece], e16))

    quarter_w, quarter_m = pl.ds(rhs * (B // X), B // X), pl.ds(rhs * (B // 2 // X), B // 2 // X)

    def weight_z():
        return [
            remote(m_send.at[quarter_m], m_x.at[quarter_m], wz_send.at[0], wz_recv.at[0], e16),
            remote(lw.at[4, quarter_w], w_x.at[quarter_w], wz_send.at[1], wz_recv.at[1], e16),
            remote(pairing_any, pair_v, wz_send.at[2], wz_recv.at[2], e16),
        ]

    def weight_x(which):
        ref, quarter = ((m_x, quarter_m), (w_x, quarter_w))[which]
        return [remote(ref.at[quarter], ref.at[quarter], wx_send.at[which, k], wx_recv.at[which, k], me, far_x[k])
                for k in range(X - 1)]

    low_w = lax.broadcasted_iota(jnp.int32, (K, 2 * K), 1) < K
    low_t = lax.broadcasted_iota(jnp.int32, (H, 2 * K), 1) < K

    def turned(x):
        return jnp.concatenate([x[:, K:], x[:, :K]], axis=1)

    def lo(x):
        return jnp.where(low_w, x, jnp.zeros_like(x))

    def hi(x):
        return jnp.where(low_w, jnp.zeros_like(x), x)

    def first_rows(pair):
        return jnp.concatenate([lo(pair), hi(pair)], axis=1)

    def second_rows(pair):
        back = turned(pair)
        return jnp.concatenate([hi(back), lo(back)], axis=1)

    def times(x, *rows):
        weight = jnp.concatenate(rows, axis=0)
        return lax.dot_general(x, weight, (((1,), (1,)), ((), ())), preferred_element_type=jnp.float32)

    def beside(own, far):
        return jnp.concatenate([own, far], axis=1)

    def bf16(x):
        return x.astype(jnp.bfloat16)

    def gathered(ref, p, half):
        tile = ref[(p // 32) * 16 + p % 16]
        return jnp.where((p // 16) % 2 == half, tile, turned(tile))

    def pair_level(l, q, i, b, swap=False):
        far = jnp.where(low_t, gathered(far_of[l][q], pairing[l, 0, b + 16], 0),
                        gathered(far_of[l][q], pairing[l, 0, b], 1))
        rows = first_rows(w[l, b]), second_rows(w[l, b + 16])
        return bf16(times(beside(state[l][q][i], far), *(rows[::-1] if swap else rows)))

    def begin(q):
        @pl.loop(0, PIECES)
        def _(piece):
            for j in range(PT):
                b = piece * 2 * PT + j
                s0[q][piece * PT + j] = beside(x_in[b, q * H:(q + 1) * H, :], x_in[b + 16, q * H:(q + 1) * H, :])
            level_copy(0, q, piece).start()

    def wait_level(l, q):
        @pl.loop(0, PIECES)
        def _(piece):
            level_copy(l, q, piece).wait_recv()

    def plain_level(l, q):
        @pl.loop(0, PIECES)
        def _(piece):
            for j in range(PT):
                i, b = piece * PT + j, piece * 2 * PT + j
                new = pair_level(l, q, i, b)
                if l < LEVELS - 1:
                    state[l + 1][q][i] = new
                else:
                    y_out[b, q * H:(q + 1) * H, :] = new[:, :K]
                    y_out[b + 16, q * H:(q + 1) * H, :] = new[:, K:]
            if l < LEVELS - 1:
                level_copy(l + 1, q, piece).start()

    def last_source_level(q):
        @pl.loop(0, PIECES)
        def _(step):
            piece = (step + z // 4) % PIECES
            for j in range(PT):
                i, b = piece * PT + j, piece * 2 * PT + j
                s4[q][i] = pair_level(3, q, i, b, swap=q % 2 == 1)

            @pl.loop(0, PT)
            def _(j):
                i = piece * PT + j
                e = piece * 2 * PT + j + 16 * (q % 2)

                @pl.when(e != me)
                def _():
                    a2a_copy(q, i, e).start()

                @pl.when(e == me)
                def _():
                    a2a_own(q, i).start()

    def middle_and_level4(q):
        a2a_recv_all(q).wait_recv()
        a2a_own(q, 0).wait()

        @pl.loop(0, 2)
        def _(part):
            for j in range(B // 4):
                d = part * (B // 4) + j
                theirs = m_x[d]
                zero = jnp.zeros((K, K), jnp.bfloat16)
                for s, other in ((d, hi(theirs)), (d + B // 2, hi(turned(theirs)))):
                    t4[q][s] = bf16(times(moved[q][s], beside(m[s], zero), other))

        @pl.loop(0, PIECES)
        def _(piece):
            for j in range(PT):
                i, first = piece * PT + j, piece * 2 * PT + j
                new = []
                for b, swap in ((first, False), (first + 16, True)):
                    far = jnp.where(low_t, t4[q][pair_s[4, 0, b]], t4[q][pairing[4, 0, b]])
                    rows = first_rows(w[4, b]), second_rows(w_x[b])
                    new.append(times(beside(t4[q][b], far), *(rows[::-1] if swap else rows)))
                s5[q][i] = bf16(jnp.where(low_t, new[0], new[1]))
                other5[q][i] = turned(bf16(jnp.where(low_t, new[1], new[0])))
            for copy in (far5_copy(q, piece),) + other_copies(q, piece):
                copy.start()

    def wait_level5(q):
        @pl.loop(0, PIECES)
        def _(piece):
            far5_copy(q, piece).wait_recv()

        @pl.when(zb1 != q % 2)
        def _():
            @pl.loop(0, PIECES)
            def _(piece):
                other_copies(q, piece)[1].wait_recv()

    waited = set()

    def need(*names):
        for name in names:
            if name not in waited:
                waited.add(name)
                if name == "m":
                    load_m.wait()
                elif name == "x":
                    for which in range(2):
                        for copy in weight_x(which):
                            copy.wait_recv()
                    to_smem = pltpu.make_async_copy(pair_v, pair_s, pair_sem)
                    to_smem.start()
                    to_smem.wait()
                else:
                    load_w[name].wait()

    def forward():
        for which, crossing in enumerate(weight_z()):
            crossing.wait_recv()
            if which < 2:
                for copy in weight_x(which):
                    copy.start()

    def store(q):
        rows = pl.ds(q * H, H)
        return pltpu.make_async_copy(y_out.at[:, rows], out.at[:, rows], out_sem.at[q])

    def task(t, q):
        if t == 4:
            need("m", "x", 4)

            @pl.when(zb1 == q % 2)
            def _():
                middle_and_level4(q)
        else:
            need(t)
            if t == 5:
                wait_level5(q)
            else:
                wait_level(t, q)
            if t == 3:
                last_source_level(q)
            else:
                plain_level(t, q)
            if t == 7:
                store(q).start()

    load_x.wait()
    pl.semaphore_wait(barrier, N - 1 + X - 1)
    for q in range(Q):
        begin(q)
    need("m")
    for d in range(B // 2):
        m_send[d] = beside(m[d + B // 2], m[d])
    for copy in weight_z():
        copy.start()
    for t in range(LEVELS):
        for q in range(Q):
            task(t, q)
            if (t, q) == (1, Q - 1):
                forward()

    for copy in weight_z() + weight_x(0) + weight_x(1):
        copy.wait_send()
    for q in range(Q):
        @pl.loop(0, PIECES)
        def _(piece):
            for l in (0, 1, 2, 3, 6, 7):
                level_copy(l, q, piece).wait_send()

        @pl.when(zb1 == q % 2)
        def _():
            @pl.loop(0, PIECES)
            def _(piece):
                for copy in (far5_copy(q, piece),) + other_copies(q, piece):
                    copy.wait_send()
            a2a_send_all(q, T - 1).wait_send()

        @pl.when(zb1 != q % 2)
        def _():
            a2a_send_all(q, T).wait_send()
    for q in range(Q):
        store(q).wait()


def body(coefficients, pairing, level_weights, middle_weights):
    bf16 = jnp.bfloat16
    dma = pltpu.SemaphoreType.DMA
    any_space = pl.BlockSpec(memory_space=pl.ANY)
    tiles = pltpu.VMEM((T, H, 2 * K), bf16)
    slots = pltpu.VMEM((B, H, 2 * K), bf16)
    return pl.pallas_call(
        kernel,
        out_shape=jax.ShapeDtypeStruct((B, C, K), bf16),
        in_specs=[any_space, pl.BlockSpec(memory_space=pltpu.SMEM), any_space, any_space, any_space],
        out_specs=any_space,
        scratch_shapes=[
            pltpu.VMEM((B, C, K), bf16),
            pltpu.VMEM((LEVELS, B, K, 2 * K), bf16),
            pltpu.VMEM((B, K, K), bf16),
            pltpu.VMEM((B, K, 2 * K), bf16),
            pltpu.VMEM((B // 2, K, 2 * K), bf16),
            pltpu.VMEM((B // 2, K, 2 * K), bf16),
            pltpu.VMEM((LEVELS, 1, B), jnp.int32),
            pltpu.SMEM((LEVELS, 1, B), jnp.int32),
            pltpu.VMEM((B, C, K), bf16),
            dma, dma((LEVELS,)), dma, dma((Q,)), dma, dma((Q,)),
            dma((LEVELS, Q, PIECES)), dma((LEVELS, Q, PIECES)), dma((Q,)), dma((Q,)),
            dma((3, Q, PIECES)), dma((2, Q, PIECES)), dma((3,)), dma((3,)), dma((2, X - 1)), dma((2, X - 1)),
        ] + [tiles] * (16 * Q) + [slots] * (2 * Q),
        compiler_params=pltpu.CompilerParams(
            collective_id=0, has_side_effects=True, vmem_limit_bytes=60 * 1024 * 1024),
    )(coefficients, pairing, pairing, level_weights, middle_weights)


def solution(mesh):
    placed = (
        P("src", "rhs", None),
        P(None, "src", None),
        P(None, "src", None, None),
        P("src", None, None),
    )
    return jax.shard_map(
        body, mesh=mesh, in_specs=placed, out_specs=P("src", "rhs", None), check_vma=False
    )
```

```python
import jax
import jax.numpy as jnp
from jax import lax
from jax.experimental import pallas as pl
from jax.experimental.pallas import tpu as pltpu
from jax.sharding import PartitionSpec as P

LEVELS = 8
N = 64
B = 64
K = 64
C = 64
Q = 4
H = C // Q
T = B // 2
PIECES = 2
PT = T // PIECES
X = 4
MESH = pl.DeviceIdType.MESH
M_PARTS, W_PARTS = 2, 4
ORDER = (
    (0, 0), (0, 1), (0, 2), (0, 3), (1, 0), (None, 0), (1, 1), (None, 1), (1, 2), (None, 2), (1, 3), (None, 3),
    (2, 0), (None, 4), (2, 1), (None, 5), (2, 2), (2, 3), (3, 0), (3, 1), (3, 2), (3, 3), (4, 0), (4, 1), (4, 2), (4, 3),
    (5, 0), (5, 1), (6, 0), (6, 1), (5, 2), (5, 3), (6, 2), (6, 3), (7, 0), (7, 1), (7, 2), (7, 3),
)
GATES = {}
GATE5 = False


def kernel(coef, pairing, pairing_any, lw, mw, out,
           x_in, w, m, w_x, m_x, m_send, pair_v, pair_s, y_out,
           in_sem, w_sem, m_sem, out_sem, pair_sem, own_sem,
           lvl_send, lvl_recv, a_send, a_recv, e_send, e_recv, wz_send, wz_recv, wx_send, wx_recv, pz_sem,
           *per_chunk):
    me = lax.axis_index("src")
    rhs = lax.axis_index("rhs")
    z = me // 8
    zb1 = (z // 2) % 2

    lists = [per_chunk[i * Q:(i + 1) * Q] for i in range(len(per_chunk) // Q)]
    s0, s1, s2, s3, s4, s5, s6, s7, r0, r1, r2, r3, r5, r6, r7, other5, moved, t4 = lists
    state, far_of = (s0, s1, s2, s3, s4, s5, s6, s7), (r0, r1, r2, r3, None, r5, r6, r7)

    load_x = pltpu.make_async_copy(coef, x_in, in_sem)
    load_x.start()
    load_w = [pltpu.make_async_copy(lw.at[l], w.at[l], w_sem.at[l]) for l in range(LEVELS)]
    load_m = pltpu.make_async_copy(mw, m, m_sem)
    load_m.start()

    def flipped(s, h):
        return s + (1 << h) * (1 - 2 * ((s // (1 << h)) % 2))

    e16, e32 = flipped(me, 4), flipped(me, 5)
    e48 = flipped(e16, 5)
    far_x = [(rhs + k) % X for k in range(1, X)]
    barrier = pltpu.get_barrier_semaphore()

    @pl.loop(1, N)
    def _(k):
        pl.semaphore_signal(barrier, inc=1, device_id=((me + k) % N, rhs), device_id_type=MESH)

    for x in far_x:
        pl.semaphore_signal(barrier, inc=1, device_id=(me, x), device_id_type=MESH)
    for l in range(LEVELS):
        load_w[l].start()

    def remote(src, dst, send, recv, dev, x=None):
        return pltpu.make_async_remote_copy(
            src_ref=src, dst_ref=dst, send_sem=send, recv_sem=recv,
            device_id=(dev, rhs if x is None else x), device_id_type=MESH)

    def level_copy(l, q, piece):
        tiles = pl.ds(piece * PT, PT)
        return remote(state[l][q].at[tiles], far_of[l][q].at[tiles],
                      lvl_send.at[l, q, piece], lvl_recv.at[l, q, piece], flipped(me, l % 6))

    def a2a_copy(q, i, e):
        return remote(s4[q].at[i], moved[q].at[me], a_send.at[q], a_recv.at[q], e)

    def a2a_own(q, i):
        return pltpu.make_async_copy(s4[q].at[i], moved[q].at[me], own_sem.at[q])

    def a2a_recv_all(q):
        return remote(moved[q].at[pl.ds(0, N - 1)], moved[q].at[pl.ds(0, N - 1)], a_send.at[q], a_recv.at[q], e16)

    def a2a_send_all(q, n):
        return remote(s4[q].at[pl.ds(0, n)], s4[q].at[pl.ds(0, n)], a_send.at[q], a_recv.at[q], e16)

    def far5_copy(q, piece):
        tiles = pl.ds(piece * PT, PT)
        return remote(s5[q].at[tiles], r5[q].at[tiles], e_send.at[0, q, piece], e_recv.at[0, q, piece], e32)

    def other_copies(q, piece):
        tiles = pl.ds(piece * PT, PT)
        src = other5[q].at[tiles]
        return (remote(src, r5[q].at[tiles], e_send.at[1, q, piece], e_recv.at[0, q, piece], e48),
                remote(src, s5[q].at[tiles], e_send.at[2, q, piece], e_recv.at[1, q, piece], e16))

    def weight_part(part):
        if part < M_PARTS:
            blocks = T // X // M_PARTS
            return m_send, m_x, pl.ds(rhs * (T // X) + part * blocks, blocks)
        blocks = B // X // W_PARTS
        return lw.at[4], w_x, pl.ds(rhs * (B // X) + (part - M_PARTS) * blocks, blocks)

    def weight_z(part):
        src, dst, blocks = weight_part(part)
        return remote(src.at[blocks], dst.at[blocks], wz_send.at[part], wz_recv.at[part], e16)

    def weight_x(part):
        _, ref, blocks = weight_part(part)
        return [remote(ref.at[blocks], ref.at[blocks], wx_send.at[part, k], wx_recv.at[part, k], me, far_x[k])
                for k in range(X - 1)]

    def pairing_z():
        return remote(pairing_any, pair_v, pz_sem.at[0], pz_sem.at[1], e16)

    low_w = lax.broadcasted_iota(jnp.int32, (K, 2 * K), 1) < K
    low_t = lax.broadcasted_iota(jnp.int32, (H, 2 * K), 1) < K

    def turned(x):
        return jnp.concatenate([x[:, K:], x[:, :K]], axis=1)

    def lo(x):
        return jnp.where(low_w, x, jnp.zeros_like(x))

    def hi(x):
        return jnp.where(low_w, jnp.zeros_like(x), x)

    def first_rows(pair):
        return jnp.concatenate([lo(pair), hi(pair)], axis=1)

    def second_rows(pair):
        back = turned(pair)
        return jnp.concatenate([hi(back), lo(back)], axis=1)

    def times(x, *rows):
        weight = jnp.concatenate(rows, axis=0)
        return lax.dot_general(x, weight, (((1,), (1,)), ((), ())), preferred_element_type=jnp.float32)

    def beside(own, far):
        return jnp.concatenate([own, far], axis=1)

    def bf16(x):
        return x.astype(jnp.bfloat16)

    def gathered(ref, p, half):
        tile = ref[(p // 32) * 16 + p % 16]
        return jnp.where((p // 16) % 2 == half, tile, turned(tile))

    def pair_level(l, q, i, b, swap=False):
        far = jnp.where(low_t, gathered(far_of[l][q], pairing[l, 0, b + 16], 0),
                        gathered(far_of[l][q], pairing[l, 0, b], 1))
        rows = first_rows(w[l, b]), second_rows(w[l, b + 16])
        return bf16(times(beside(state[l][q][i], far), *(rows[::-1] if swap else rows)))

    def begin(q):
        @pl.loop(0, PIECES)
        def _(piece):
            for j in range(PT):
                b = piece * 2 * PT + j
                s0[q][piece * PT + j] = beside(x_in[b, q * H:(q + 1) * H, :], x_in[b + 16, q * H:(q + 1) * H, :])
            level_copy(0, q, piece).start()

    def wait_level(l, q):
        @pl.loop(0, PIECES)
        def _(piece):
            level_copy(l, q, piece).wait_recv()

    left = set()

    def wait_sent(l, q):
        if (l, q) not in left:
            left.add((l, q))

            @pl.loop(0, PIECES)
            def _(piece):
                level_copy(l, q, piece).wait_send()

    def plain_level(l, q):
        held = (l + 1, q) in GATES

        @pl.loop(0, PIECES)
        def _(piece):
            for j in range(PT):
                i, b = piece * PT + j, piece * 2 * PT + j
                new = pair_level(l, q, i, b)
                if l < LEVELS - 1:
                    state[l + 1][q][i] = new
                else:
                    y_out[b, q * H:(q + 1) * H, :] = new[:, :K]
                    y_out[b + 16, q * H:(q + 1) * H, :] = new[:, K:]
            if l < LEVELS - 1 and not held:
                level_copy(l + 1, q, piece).start()

        if held:
            wait_sent(*GATES[l + 1, q])

            @pl.loop(0, PIECES)
            def _(piece):
                level_copy(l + 1, q, piece).start()

    def last_source_level(q):
        @pl.loop(0, PIECES)
        def _(step):
            piece = (step + z // 4) % PIECES
            for j in range(PT):
                i, b = piece * PT + j, piece * 2 * PT + j
                s4[q][i] = pair_level(3, q, i, b, swap=q % 2 == 1)

            @pl.loop(0, PT)
            def _(j):
                i = piece * PT + j
                e = piece * 2 * PT + j + 16 * (q % 2)

                @pl.when(e != me)
                def _():
                    a2a_copy(q, i, e).start()

                @pl.when(e == me)
                def _():
                    a2a_own(q, i).start()

    def middle(q):
        a2a_recv_all(q).wait_recv()
        a2a_own(q, 0).wait()

        @pl.loop(0, 2)
        def _(part):
            for j in range(B // 4):
                d = part * (B // 4) + j
                theirs = m_x[d]
                zero = jnp.zeros((K, K), jnp.bfloat16)
                for s, other in ((d, hi(theirs)), (d + B // 2, hi(turned(theirs)))):
                    t4[q][s] = bf16(times(moved[q][s], beside(m[s], zero), other))

    def send_level5(q, piece):
        for copy in (far5_copy(q, piece),) + other_copies(q, piece):
            copy.start()

    def wait_sent5(q):
        if (5, q) not in left:
            left.add((5, q))

            @pl.loop(0, PIECES)
            def _(piece):
                for copy in (far5_copy(q, piece),) + other_copies(q, piece):
                    copy.wait_send()

    def level4(q):
        held = GATE5 and q >= 2

        @pl.loop(0, PIECES)
        def _(piece):
            for j in range(PT):
                i, first = piece * PT + j, piece * 2 * PT + j
                new = []
                for b, swap in ((first, False), (first + 16, True)):
                    far = jnp.where(low_t, t4[q][pair_s[4, 0, b]], t4[q][pairing[4, 0, b]])
                    rows = first_rows(w[4, b]), second_rows(w_x[b])
                    new.append(times(beside(t4[q][b], far), *(rows[::-1] if swap else rows)))
                s5[q][i] = bf16(jnp.where(low_t, new[0], new[1]))
                other5[q][i] = turned(bf16(jnp.where(low_t, new[1], new[0])))
            if not held:
                send_level5(q, piece)

        if held:
            wait_sent5(q - 2)

            @pl.loop(0, PIECES)
            def _(piece):
                send_level5(q, piece)

    def wait_level5(q):
        @pl.loop(0, PIECES)
        def _(piece):
            far5_copy(q, piece).wait_recv()

        @pl.when(zb1 != q % 2)
        def _():
            @pl.loop(0, PIECES)
            def _(piece):
                other_copies(q, piece)[1].wait_recv()

    waited = set()

    def need(*names):
        for name in names:
            if name not in waited:
                waited.add(name)
                if name == "m of e16":
                    for part in range(M_PARTS):
                        for copy in weight_x(part):
                            copy.wait_recv()
                elif name == "w of e16":
                    for part in range(M_PARTS, M_PARTS + W_PARTS):
                        for copy in weight_x(part):
                            copy.wait_recv()
                    pairing_z().wait_recv()
                    to_smem = pltpu.make_async_copy(pair_v, pair_s, pair_sem)
                    to_smem.start()
                    to_smem.wait()
                else:
                    load_w[name].wait()

    def forward(part):
        weight_z(part).wait_recv()
        for copy in weight_x(part):
            copy.start()

    def store(q):
        rows = pl.ds(q * H, H)
        return pltpu.make_async_copy(y_out.at[:, rows], out.at[:, rows], out_sem.at[q])

    def task(t, q):
        if t == 4:
            need("m of e16")

            @pl.when(zb1 == q % 2)
            def _():
                middle(q)

            need("w of e16", 4)

            @pl.when(zb1 == q % 2)
            def _():
                level4(q)
        else:
            need(t)
            if t == 5:
                wait_level5(q)
            else:
                wait_level(t, q)
            if t == 3:
                last_source_level(q)
            else:
                plain_level(t, q)
            if t == 7:
                store(q).start()

    load_m.wait()
    for d in range(T):
        m_send[d] = beside(m[d + T], m[d])
    load_x.wait()
    pl.semaphore_wait(barrier, N - 1 + X - 1)
    begin(0)
    for part in range(M_PARTS + W_PARTS):
        weight_z(part).start()
    pairing_z().start()
    for q in range(1, Q):
        begin(q)
    for t, q in ORDER:
        if t is None:
            forward(q)
        else:
            task(t, q)

    pairing_z().wait_send()
    for part in range(M_PARTS + W_PARTS):
        for copy in [weight_z(part)] + weight_x(part):
            copy.wait_send()
    for q in range(Q):
        for l in (0, 1, 2, 3, 6, 7):
            wait_sent(l, q)

        @pl.when(zb1 == q % 2)
        def _():
            wait_sent5(q)
            a2a_send_all(q, T - 1).wait_send()

        @pl.when(zb1 != q % 2)
        def _():
            a2a_send_all(q, T).wait_send()
    for q in range(Q):
        store(q).wait()


def body(coefficients, pairing, level_weights, middle_weights):
    bf16 = jnp.bfloat16
    dma = pltpu.SemaphoreType.DMA
    PARTS = M_PARTS + W_PARTS
    any_space = pl.BlockSpec(memory_space=pl.ANY)
    tiles = pltpu.VMEM((T, H, 2 * K), bf16)
    slots = pltpu.VMEM((B, H, 2 * K), bf16)
    return pl.pallas_call(
        kernel,
        out_shape=jax.ShapeDtypeStruct((B, C, K), bf16),
        in_specs=[any_space, pl.BlockSpec(memory_space=pltpu.SMEM), any_space, any_space, any_space],
        out_specs=any_space,
        scratch_shapes=[
            pltpu.VMEM((B, C, K), bf16),
            pltpu.VMEM((LEVELS, B, K, 2 * K), bf16),
            pltpu.VMEM((B, K, K), bf16),
            pltpu.VMEM((B, K, 2 * K), bf16),
            pltpu.VMEM((B // 2, K, 2 * K), bf16),
            pltpu.VMEM((B // 2, K, 2 * K), bf16),
            pltpu.VMEM((LEVELS, 1, B), jnp.int32),
            pltpu.SMEM((LEVELS, 1, B), jnp.int32),
            pltpu.VMEM((B, C, K), bf16),
            dma, dma((LEVELS,)), dma, dma((Q,)), dma, dma((Q,)),
            dma((LEVELS, Q, PIECES)), dma((LEVELS, Q, PIECES)), dma((Q,)), dma((Q,)),
            dma((3, Q, PIECES)), dma((2, Q, PIECES)), dma((PARTS,)), dma((PARTS,)), dma((PARTS, X - 1)), dma((PARTS, X - 1)), dma((2,)),
        ] + [tiles] * (16 * Q) + [slots] * (2 * Q),
        compiler_params=pltpu.CompilerParams(
            collective_id=0, has_side_effects=True, vmem_limit_bytes=52 * 1024 * 1024),
    )(coefficients, pairing, pairing, level_weights, middle_weights)


def solution(mesh):
    placed = (
        P("src", "rhs", None),
        P(None, "src", None),
        P(None, "src", None, None),
        P("src", None, None),
    )
    return jax.shard_map(
        body, mesh=mesh, in_specs=placed, out_specs=P("src", "rhs", None), check_vma=False
    )
```

```python
import jax
import jax.numpy as jnp
from jax import lax
from jax.experimental import pallas as pl
from jax.experimental.pallas import tpu as pltpu
from jax.sharding import PartitionSpec as P

LEVELS = 8
N = 64
B = 64
K = 64
C = 64
Q = 4
H = C // Q
T = B // 2
PIECES = 2
PT = T // PIECES
X = 4
MESH = pl.DeviceIdType.MESH
M_PARTS, W_PARTS = 2, 4
ORDER = (
    (0, (0,)), (0, (1,)), (0, (2,)), (0, (3,)),
    (1, (0,)), (None, 0), (1, (1,)), (None, 1), (1, (2,)), (None, 2), (1, (3,)), (None, 3),
    (2, (0,)), (None, 4), (2, (1,)), (None, 5), (2, (2,)), (2, (3,)),
    (3, (0,)), (3, (1,)), (3, (2,)), (3, (3,)),
    (4, (0,)), (4, (1,)), (4, (2,)), (4, (3,)),
    (5, (0,)), (6, (0,)), (5, (1,)), (6, (1,)), (5, (2,)), (6, (2,)), (5, (3,)), (6, (3,)),
    (7, (0,)), (7, (1,)), (7, (2,)), (7, (3,)),
)


def kernel(coef, pairing, pairing_any, lw, mw, out,
           x_in, w, m, w_x, m_x, m_send, pair_v, pair_s, y_out,
           in_sem, w_sem, m_sem, out_sem, pair_sem, own_sem,
           lvl_send, lvl_recv, a_send, a_recv, e_send, e_recv, wz_send, wz_recv, wx_send, wx_recv, pz_sem,
           *per_chunk):
    me = lax.axis_index("src")
    rhs = lax.axis_index("rhs")
    z = me // 8
    zb1 = (z // 2) % 2

    lists = [per_chunk[i * Q:(i + 1) * Q] for i in range(len(per_chunk) // Q)]
    s0, s1, s2, s3, s4, s5, s6, s7, r0, r1, r2, r3, r5, r6, r7, other5, moved, t4 = lists
    state, far_of = (s0, s1, s2, s3, s4, s5, s6, s7), (r0, r1, r2, r3, None, r5, r6, r7)

    load_x = pltpu.make_async_copy(coef, x_in, in_sem)
    load_x.start()
    load_w = [pltpu.make_async_copy(lw.at[l], w.at[l], w_sem.at[l]) for l in range(LEVELS)]
    load_m = pltpu.make_async_copy(mw, m, m_sem)
    load_m.start()

    def flipped(s, h):
        return s + (1 << h) * (1 - 2 * ((s // (1 << h)) % 2))

    e16, e32 = flipped(me, 4), flipped(me, 5)
    e48 = flipped(e16, 5)
    far_x = [(rhs + k) % X for k in range(1, X)]
    barrier = pltpu.get_barrier_semaphore()

    @pl.loop(1, N)
    def _(k):
        pl.semaphore_signal(barrier, inc=1, device_id=((me + k) % N, rhs), device_id_type=MESH)

    for x in far_x:
        pl.semaphore_signal(barrier, inc=1, device_id=(me, x), device_id_type=MESH)
    for l in range(LEVELS):
        load_w[l].start()

    def remote(src, dst, send, recv, dev, x=None):
        return pltpu.make_async_remote_copy(
            src_ref=src, dst_ref=dst, send_sem=send, recv_sem=recv,
            device_id=(dev, rhs if x is None else x), device_id_type=MESH)

    def level_copy(l, q, piece):
        tiles = pl.ds(piece * PT, PT)
        return remote(state[l][q].at[tiles], far_of[l][q].at[tiles],
                      lvl_send.at[l, q, piece], lvl_recv.at[l, q, piece], flipped(me, l % 6))

    def a2a_copy(q, i, e):
        return remote(s4[q].at[i], moved[q].at[me], a_send.at[q], a_recv.at[q], e)

    def a2a_own(q, i):
        return pltpu.make_async_copy(s4[q].at[i], moved[q].at[me], own_sem.at[q])

    def a2a_recv_all(q):
        return remote(moved[q].at[pl.ds(0, N - 1)], moved[q].at[pl.ds(0, N - 1)], a_send.at[q], a_recv.at[q], e16)

    def a2a_send_all(q, n):
        return remote(s4[q].at[pl.ds(0, n)], s4[q].at[pl.ds(0, n)], a_send.at[q], a_recv.at[q], e16)

    def far5_copy(q, piece):
        tiles = pl.ds(piece * PT, PT)
        return remote(s5[q].at[tiles], r5[q].at[tiles], e_send.at[0, q, piece], e_recv.at[0, q, piece], e32)

    def other_copies(q, piece):
        tiles = pl.ds(piece * PT, PT)
        src = other5[q].at[tiles]
        return (remote(src, r5[q].at[tiles], e_send.at[1, q, piece], e_recv.at[0, q, piece], e48),
                remote(src, s5[q].at[tiles], e_send.at[2, q, piece], e_recv.at[1, q, piece], e16))

    def weight_part(part):
        if part < M_PARTS:
            blocks = T // X // M_PARTS
            return m_send, m_x, pl.ds(rhs * (T // X) + part * blocks, blocks)
        blocks = B // X // W_PARTS
        return lw.at[4], w_x, pl.ds(rhs * (B // X) + (part - M_PARTS) * blocks, blocks)

    def weight_z(part):
        src, dst, blocks = weight_part(part)
        return remote(src.at[blocks], dst.at[blocks], wz_send.at[part], wz_recv.at[part], e16)

    def weight_x(part):
        _, ref, blocks = weight_part(part)
        return [remote(ref.at[blocks], ref.at[blocks], wx_send.at[part, k], wx_recv.at[part, k], me, far_x[k])
                for k in range(X - 1)]

    def pairing_z():
        return remote(pairing_any, pair_v, pz_sem.at[0], pz_sem.at[1], e16)

    low_w = lax.broadcasted_iota(jnp.int32, (K, 2 * K), 1) < K
    low_t = lax.broadcasted_iota(jnp.int32, (H, 2 * K), 1) < K

    def turned(x):
        return jnp.concatenate([x[:, K:], x[:, :K]], axis=1)

    def lo(x):
        return jnp.where(low_w, x, jnp.zeros_like(x))

    def hi(x):
        return jnp.where(low_w, jnp.zeros_like(x), x)

    def first_rows(pair):
        return jnp.concatenate([lo(pair), hi(pair)], axis=1)

    def second_rows(pair):
        back = turned(pair)
        return jnp.concatenate([hi(back), lo(back)], axis=1)

    def times(x, *rows):
        weight = jnp.concatenate(rows, axis=0)
        return lax.dot_general(x, weight, (((1,), (1,)), ((), ())), preferred_element_type=jnp.float32)

    def beside(own, far):
        return jnp.concatenate([own, far], axis=1)

    def bf16(x):
        return x.astype(jnp.bfloat16)

    def gathered(ref, p, half):
        tile = ref[((p >> 5) << 4) | (p & 15)]
        return jnp.where(((p >> 4) & 1) == half, tile, turned(tile))

    def pair_level(l, qs, i, b):
        first, second = pairing[l, 0, b], pairing[l, 0, b + 16]
        tiles = []
        for q in qs:
            far = jnp.where(low_t, gathered(far_of[l][q], second, 0), gathered(far_of[l][q], first, 1))
            tiles.append(beside(state[l][q][i], far))
        new = bf16(times(jnp.concatenate(tiles, axis=0), first_rows(w[l, b]), second_rows(w[l, b + 16])))
        return [new[k * H:(k + 1) * H] for k in range(len(qs))]

    def pack(q):
        @pl.loop(0, PIECES)
        def _(piece):
            for j in range(PT):
                b = piece * 2 * PT + j
                s0[q][piece * PT + j] = beside(x_in[b, q * H:(q + 1) * H, :], x_in[b + 16, q * H:(q + 1) * H, :])

    def send_first(q):
        @pl.loop(0, PIECES)
        def _(piece):
            level_copy(0, q, piece).start()

    def wait_level(l, q):
        @pl.loop(0, PIECES)
        def _(piece):
            level_copy(l, q, piece).wait_recv()

    def plain_level(l, qs):
        @pl.loop(0, PIECES)
        def _(piece):
            for j in range(PT):
                i, b = piece * PT + j, piece * 2 * PT + j
                for q, new in zip(qs, pair_level(l, qs, i, b)):
                    if l < LEVELS - 1:
                        state[l + 1][q][i] = new
                    else:
                        y_out[b, q * H:(q + 1) * H, :] = new[:, :K]
                        y_out[b + 16, q * H:(q + 1) * H, :] = new[:, K:]
            if l < LEVELS - 1:
                for q in qs:
                    level_copy(l + 1, q, piece).start()

    def last_source_level(qs):
        @pl.loop(0, PIECES)
        def _(step):
            piece = (step + z // 4) % PIECES
            for j in range(PT):
                i, b = piece * PT + j, piece * 2 * PT + j
                for q, new in zip(qs, pair_level(3, qs, i, b)):
                    s4[q][i] = turned(new) if q % 2 else new

            @pl.loop(0, PT)
            def _(j):
                i = piece * PT + j
                for q in qs:
                    e = piece * 2 * PT + j + 16 * (q % 2)

                    @pl.when(e != me)
                    def _():
                        a2a_copy(q, i, e).start()

                    @pl.when(e == me)
                    def _():
                        a2a_own(q, i).start()

    def middle(q):
        a2a_recv_all(q).wait_recv()
        a2a_own(q, 0).wait()

        @pl.loop(0, 2)
        def _(part):
            for j in range(B // 4):
                d = part * (B // 4) + j
                theirs = m_x[d]
                zero = jnp.zeros((K, K), jnp.bfloat16)
                for s, other in ((d, hi(theirs)), (d + B // 2, hi(turned(theirs)))):
                    t4[q][s] = bf16(times(moved[q][s], beside(m[s], zero), other))

    def level4(q):
        @pl.loop(0, PIECES)
        def _(piece):
            for j in range(PT):
                i, first = piece * PT + j, piece * 2 * PT + j
                new = []
                for b, swap in ((first, False), (first + 16, True)):
                    far = jnp.where(low_t, t4[q][pair_s[4, 0, b]], t4[q][pairing[4, 0, b]])
                    rows = first_rows(w[4, b]), second_rows(w_x[b])
                    new.append(times(beside(t4[q][b], far), *(rows[::-1] if swap else rows)))
                s5[q][i] = bf16(jnp.where(low_t, new[0], new[1]))
                other5[q][i] = turned(bf16(jnp.where(low_t, new[1], new[0])))
            for copy in (far5_copy(q, piece),) + other_copies(q, piece):
                copy.start()

    def wait_level5(q):
        @pl.loop(0, PIECES)
        def _(piece):
            far5_copy(q, piece).wait_recv()

        @pl.when(zb1 != q % 2)
        def _():
            @pl.loop(0, PIECES)
            def _(piece):
                other_copies(q, piece)[1].wait_recv()

    waited = set()

    def need(*names):
        for name in names:
            if name not in waited:
                waited.add(name)
                if name == "m of e16":
                    for part in range(M_PARTS):
                        for copy in weight_x(part):
                            copy.wait_recv()
                elif name == "w of e16":
                    for part in range(M_PARTS, M_PARTS + W_PARTS):
                        for copy in weight_x(part):
                            copy.wait_recv()
                    pairing_z().wait_recv()
                    to_smem = pltpu.make_async_copy(pair_v, pair_s, pair_sem)
                    to_smem.start()
                    to_smem.wait()
                else:
                    load_w[name].wait()

    def forward(part):
        weight_z(part).wait_recv()
        for copy in weight_x(part):
            copy.start()

    def store(q):
        rows = pl.ds(q * H, H)
        return pltpu.make_async_copy(y_out.at[:, rows], out.at[:, rows], out_sem.at[q])

    def task(t, qs):
        if t == 4:
            need("m of e16")
            for q in qs:
                @pl.when(zb1 == q % 2)
                def _():
                    middle(q)

            need("w of e16", 4)
            for q in qs:
                @pl.when(zb1 == q % 2)
                def _():
                    level4(q)
            return
        need(t)
        for q in qs:
            if t == 5:
                wait_level5(q)
            else:
                wait_level(t, q)
        if t == 3:
            last_source_level(qs)
        else:
            plain_level(t, qs)
        if t == 7:
            for q in qs:
                store(q).start()

    load_x.wait()
    pack(0)
    pl.semaphore_wait(barrier, N - 1 + X - 1)
    send_first(0)
    for part in range(M_PARTS, M_PARTS + W_PARTS):
        weight_z(part).start()
    pairing_z().start()
    pack(1)
    send_first(1)
    load_m.wait()
    for d in range(T):
        m_send[d] = beside(m[d + T], m[d])
    for part in range(M_PARTS):
        weight_z(part).start()
    for q in range(2, Q):
        pack(q)
        send_first(q)
    for t, what in ORDER:
        if t is None:
            forward(what)
        else:
            task(t, what)

    pairing_z().wait_send()
    for part in range(M_PARTS + W_PARTS):
        for copy in [weight_z(part)] + weight_x(part):
            copy.wait_send()
    for q in range(Q):
        @pl.loop(0, PIECES)
        def _(piece):
            for l in (0, 1, 2, 3, 6, 7):
                level_copy(l, q, piece).wait_send()

        @pl.when(zb1 == q % 2)
        def _():
            @pl.loop(0, PIECES)
            def _(piece):
                for copy in (far5_copy(q, piece),) + other_copies(q, piece):
                    copy.wait_send()
            a2a_send_all(q, T - 1).wait_send()

        @pl.when(zb1 != q % 2)
        def _():
            a2a_send_all(q, T).wait_send()
    for q in range(Q):
        store(q).wait()


def body(coefficients, pairing, level_weights, middle_weights):
    bf16 = jnp.bfloat16
    dma = pltpu.SemaphoreType.DMA
    PARTS = M_PARTS + W_PARTS
    any_space = pl.BlockSpec(memory_space=pl.ANY)
    tiles = pltpu.VMEM((T, H, 2 * K), bf16)
    slots = pltpu.VMEM((B, H, 2 * K), bf16)
    return pl.pallas_call(
        kernel,
        out_shape=jax.ShapeDtypeStruct((B, C, K), bf16),
        in_specs=[any_space, pl.BlockSpec(memory_space=pltpu.SMEM), any_space, any_space, any_space],
        out_specs=any_space,
        scratch_shapes=[
            pltpu.VMEM((B, C, K), bf16),
            pltpu.VMEM((LEVELS, B, K, 2 * K), bf16),
            pltpu.VMEM((B, K, K), bf16),
            pltpu.VMEM((B, K, 2 * K), bf16),
            pltpu.VMEM((B // 2, K, 2 * K), bf16),
            pltpu.VMEM((B // 2, K, 2 * K), bf16),
            pltpu.VMEM((LEVELS, 1, B), jnp.int32),
            pltpu.SMEM((LEVELS, 1, B), jnp.int32),
            pltpu.VMEM((B, C, K), bf16),
            dma, dma((LEVELS,)), dma, dma((Q,)), dma, dma((Q,)),
            dma((LEVELS, Q, PIECES)), dma((LEVELS, Q, PIECES)), dma((Q,)), dma((Q,)),
            dma((3, Q, PIECES)), dma((2, Q, PIECES)), dma((PARTS,)), dma((PARTS,)), dma((PARTS, X - 1)), dma((PARTS, X - 1)), dma((2,)),
        ] + [tiles] * (16 * Q) + [slots] * (2 * Q),
        compiler_params=pltpu.CompilerParams(
            collective_id=0, has_side_effects=True, vmem_limit_bytes=52 * 1024 * 1024),
    )(coefficients, pairing, pairing, level_weights, middle_weights)


def solution(mesh):
    placed = (
        P("src", "rhs", None),
        P(None, "src", None),
        P(None, "src", None, None),
        P("src", None, None),
    )
    return jax.shard_map(
        body, mesh=mesh, in_specs=placed, out_specs=P("src", "rhs", None), check_vma=False
    )
```

```python
import jax
import jax.numpy as jnp
from jax import lax
from jax.experimental import pallas as pl
from jax.experimental.pallas import tpu as pltpu
from jax.sharding import PartitionSpec as P

LEVELS = 8
N = 64
B = 64
K = 64
C = 64
Q = 4
H = C // Q
T = B // 2
PIECES = 2
PT = T // PIECES
X = 4
MESH = pl.DeviceIdType.MESH
M_PARTS, W_PARTS = 2, 4
FIRST = 2
ORDER = (
    (0, (0,)), (0, (1,)), ("z", 2), ("z", 3), (0, (2,)), (0, (3,)), ("z", 4), ("z", 5),
    (1, (0,)), ("x", 0), (1, (1,)), ("x", 1), (1, (2,)), (1, (3,)), ("x", 2), ("x", 3),
    (2, (0,)), ("x", 4), (2, (1,)), ("x", 5), (2, (2,)), (2, (3,)),
    (3, (0,)), (3, (1,)), (3, (2,)), (3, (3,)),
    (4, (0,)), (4, (1,)), (4, (2,)), (4, (3,)),
    (5, (0,)), (6, (0,)), (5, (1,)), (6, (1,)), (5, (2,)), (6, (2,)), (5, (3,)), (6, (3,)),
    (7, (0,)), (7, (1,)), (7, (2,)), (7, (3,)),
)


def kernel(coef, pairing, pairing_any, lw, mw, out,
           x_in, w, m, w_x, m_x, m_send, pair_v, pair_s, y_out,
           in_sem, w_sem, m_sem, out_sem, pair_sem, own_sem,
           lvl_send, lvl_recv, a_send, a_recv, e_send, e_recv, wz_send, wz_recv, wx_send, wx_recv, pz_sem,
           *per_chunk):
    me = lax.axis_index("src")
    rhs = lax.axis_index("rhs")
    z = me // 8
    zb1 = (z // 2) % 2

    lists = [per_chunk[i * Q:(i + 1) * Q] for i in range(len(per_chunk) // Q)]
    s0, s1, s2, s3, s4, s5, s6, s7, r0, r1, r2, r3, r5, r6, r7, other5, moved, t4 = lists
    state, far_of = (s0, s1, s2, s3, s4, s5, s6, s7), (r0, r1, r2, r3, None, r5, r6, r7)

    load_x = pltpu.make_async_copy(coef, x_in, in_sem)
    load_x.start()
    load_w = [pltpu.make_async_copy(lw.at[l], w.at[l], w_sem.at[l]) for l in range(LEVELS)]
    load_m = pltpu.make_async_copy(mw, m, m_sem)
    load_m.start()

    def flipped(s, h):
        return s + (1 << h) * (1 - 2 * ((s // (1 << h)) % 2))

    e16, e32 = flipped(me, 4), flipped(me, 5)
    e48 = flipped(e16, 5)
    far_x = [(rhs + k) % X for k in range(1, X)]
    barrier = pltpu.get_barrier_semaphore()

    @pl.loop(1, N)
    def _(k):
        pl.semaphore_signal(barrier, inc=1, device_id=((me + k) % N, rhs), device_id_type=MESH)

    for x in far_x:
        pl.semaphore_signal(barrier, inc=1, device_id=(me, x), device_id_type=MESH)
    for l in range(LEVELS):
        load_w[l].start()

    def remote(src, dst, send, recv, dev, x=None):
        return pltpu.make_async_remote_copy(
            src_ref=src, dst_ref=dst, send_sem=send, recv_sem=recv,
            device_id=(dev, rhs if x is None else x), device_id_type=MESH)

    def level_copy(l, q, piece):
        tiles = pl.ds(piece * PT, PT)
        return remote(state[l][q].at[tiles], far_of[l][q].at[tiles],
                      lvl_send.at[l, q, piece], lvl_recv.at[l, q, piece], flipped(me, l % 6))

    def a2a_copy(q, i, e):
        return remote(s4[q].at[i], moved[q].at[me], a_send.at[q], a_recv.at[q], e)

    def a2a_own(q, i):
        return pltpu.make_async_copy(s4[q].at[i], moved[q].at[me], own_sem.at[q])

    def a2a_recv_all(q):
        return remote(moved[q].at[pl.ds(0, N - 1)], moved[q].at[pl.ds(0, N - 1)], a_send.at[q], a_recv.at[q], e16)

    def a2a_send_all(q, n):
        return remote(s4[q].at[pl.ds(0, n)], s4[q].at[pl.ds(0, n)], a_send.at[q], a_recv.at[q], e16)

    def far5_copy(q, piece):
        tiles = pl.ds(piece * PT, PT)
        return remote(s5[q].at[tiles], r5[q].at[tiles], e_send.at[0, q, piece], e_recv.at[0, q, piece], e32)

    def other_copies(q, piece):
        tiles = pl.ds(piece * PT, PT)
        src = other5[q].at[tiles]
        return (remote(src, r5[q].at[tiles], e_send.at[1, q, piece], e_recv.at[0, q, piece], e48),
                remote(src, s5[q].at[tiles], e_send.at[2, q, piece], e_recv.at[1, q, piece], e16))

    def weight_part(part):
        if part < M_PARTS:
            blocks = T // X // M_PARTS
            return m_send, m_x, pl.ds(rhs * (T // X) + part * blocks, blocks)
        blocks = B // X // W_PARTS
        return lw.at[4], w_x, pl.ds(rhs * (B // X) + (part - M_PARTS) * blocks, blocks)

    def weight_z(part):
        src, dst, blocks = weight_part(part)
        return remote(src.at[blocks], dst.at[blocks], wz_send.at[part], wz_recv.at[part], e16)

    def weight_x(part):
        _, ref, blocks = weight_part(part)
        return [remote(ref.at[blocks], ref.at[blocks], wx_send.at[part, k], wx_recv.at[part, k], me, far_x[k])
                for k in range(X - 1)]

    def pairing_z():
        return remote(pairing_any, pair_v, pz_sem.at[0], pz_sem.at[1], e16)

    low_w = lax.broadcasted_iota(jnp.int32, (K, 2 * K), 1) < K
    low_t = lax.broadcasted_iota(jnp.int32, (H, 2 * K), 1) < K

    def turned(x):
        return jnp.concatenate([x[:, K:], x[:, :K]], axis=1)

    def lo(x):
        return jnp.where(low_w, x, jnp.zeros_like(x))

    def hi(x):
        return jnp.where(low_w, jnp.zeros_like(x), x)

    def first_rows(pair):
        return jnp.concatenate([lo(pair), hi(pair)], axis=1)

    def second_rows(pair):
        back = turned(pair)
        return jnp.concatenate([hi(back), lo(back)], axis=1)

    def times(x, *rows):
        weight = jnp.concatenate(rows, axis=0)
        return lax.dot_general(x, weight, (((1,), (1,)), ((), ())), preferred_element_type=jnp.float32)

    def beside(own, far):
        return jnp.concatenate([own, far], axis=1)

    def bf16(x):
        return x.astype(jnp.bfloat16)

    def gathered(ref, p, half):
        tile = ref[((p >> 5) << 4) | (p & 15)]
        return jnp.where(((p >> 4) & 1) == half, tile, turned(tile))

    def pair_level(l, qs, i, b):
        first, second = pairing[l, 0, b], pairing[l, 0, b + 16]
        tiles = []
        for q in qs:
            far = jnp.where(low_t, gathered(far_of[l][q], second, 0), gathered(far_of[l][q], first, 1))
            tiles.append(beside(state[l][q][i], far))
        new = bf16(times(jnp.concatenate(tiles, axis=0), first_rows(w[l, b]), second_rows(w[l, b + 16])))
        return [new[k * H:(k + 1) * H] for k in range(len(qs))]

    def pack(q):
        @pl.loop(0, PIECES)
        def _(piece):
            for j in range(PT):
                b = piece * 2 * PT + j
                s0[q][piece * PT + j] = beside(x_in[b, q * H:(q + 1) * H, :], x_in[b + 16, q * H:(q + 1) * H, :])

    def send_first(q):
        @pl.loop(0, PIECES)
        def _(piece):
            level_copy(0, q, piece).start()

    def wait_level(l, q):
        @pl.loop(0, PIECES)
        def _(piece):
            level_copy(l, q, piece).wait_recv()

    def plain_level(l, qs):
        @pl.loop(0, PIECES)
        def _(piece):
            for j in range(PT):
                i, b = piece * PT + j, piece * 2 * PT + j
                for q, new in zip(qs, pair_level(l, qs, i, b)):
                    if l < LEVELS - 1:
                        state[l + 1][q][i] = new
                    else:
                        y_out[b, q * H:(q + 1) * H, :] = new[:, :K]
                        y_out[b + 16, q * H:(q + 1) * H, :] = new[:, K:]
            if l < LEVELS - 1:
                for q in qs:
                    level_copy(l + 1, q, piece).start()

    def last_source_level(qs):
        @pl.loop(0, PIECES)
        def _(step):
            piece = (step + z // 4) % PIECES
            for j in range(PT):
                i, b = piece * PT + j, piece * 2 * PT + j
                for q, new in zip(qs, pair_level(3, qs, i, b)):
                    s4[q][i] = turned(new) if q % 2 else new

            @pl.loop(0, PT)
            def _(j):
                i = piece * PT + j
                for q in qs:
                    e = piece * 2 * PT + j + 16 * (q % 2)

                    @pl.when(e != me)
                    def _():
                        a2a_copy(q, i, e).start()

                    @pl.when(e == me)
                    def _():
                        a2a_own(q, i).start()

    def middle(q):
        a2a_recv_all(q).wait_recv()
        a2a_own(q, 0).wait()

        @pl.loop(0, 2)
        def _(part):
            for j in range(B // 4):
                d = part * (B // 4) + j
                theirs = m_x[d]
                zero = jnp.zeros((K, K), jnp.bfloat16)
                for s, other in ((d, hi(theirs)), (d + B // 2, hi(turned(theirs)))):
                    t4[q][s] = bf16(times(moved[q][s], beside(m[s], zero), other))

    def level4(q):
        @pl.loop(0, PIECES)
        def _(piece):
            for j in range(PT):
                i, first = piece * PT + j, piece * 2 * PT + j
                new = []
                for b, swap in ((first, False), (first + 16, True)):
                    far = jnp.where(low_t, t4[q][pair_s[4, 0, b]], t4[q][pairing[4, 0, b]])
                    rows = first_rows(w[4, b]), second_rows(w_x[b])
                    new.append(times(beside(t4[q][b], far), *(rows[::-1] if swap else rows)))
                s5[q][i] = bf16(jnp.where(low_t, new[0], new[1]))
                other5[q][i] = turned(bf16(jnp.where(low_t, new[1], new[0])))
            for copy in (far5_copy(q, piece),) + other_copies(q, piece):
                copy.start()

    def wait_level5(q):
        @pl.loop(0, PIECES)
        def _(piece):
            far5_copy(q, piece).wait_recv()

        @pl.when(zb1 != q % 2)
        def _():
            @pl.loop(0, PIECES)
            def _(piece):
                other_copies(q, piece)[1].wait_recv()

    waited = set()

    def need(*names):
        for name in names:
            if name not in waited:
                waited.add(name)
                if name == "m of e16":
                    for part in range(M_PARTS):
                        for copy in weight_x(part):
                            copy.wait_recv()
                elif name == "w of e16":
                    for part in range(M_PARTS, M_PARTS + W_PARTS):
                        for copy in weight_x(part):
                            copy.wait_recv()
                    pairing_z().wait_recv()
                    to_smem = pltpu.make_async_copy(pair_v, pair_s, pair_sem)
                    to_smem.start()
                    to_smem.wait()
                else:
                    load_w[name].wait()

    def forward(part):
        weight_z(part).wait_recv()
        for copy in weight_x(part):
            copy.start()

    def store(q):
        rows = pl.ds(q * H, H)
        return pltpu.make_async_copy(y_out.at[:, rows], out.at[:, rows], out_sem.at[q])

    def task(t, qs):
        if t == 4:
            need("m of e16")
            for q in qs:
                @pl.when(zb1 == q % 2)
                def _():
                    middle(q)

            need("w of e16", 4)
            for q in qs:
                @pl.when(zb1 == q % 2)
                def _():
                    level4(q)
            return
        need(t)
        for q in qs:
            if t == 5:
                wait_level5(q)
            else:
                wait_level(t, q)
        if t == 3:
            last_source_level(qs)
        else:
            plain_level(t, qs)
        if t == 7:
            for q in qs:
                store(q).start()

    load_m.wait()
    for d in range(T):
        m_send[d] = beside(m[d + T], m[d])
    load_x.wait()
    pack(0)
    pl.semaphore_wait(barrier, N - 1 + X - 1)
    send_first(0)
    for part in range(FIRST):
        weight_z(part).start()
    pairing_z().start()
    for q in range(1, Q):
        pack(q)
        send_first(q)
    for t, what in ORDER:
        if t == "z":
            weight_z(what).start()
        elif t == "x":
            forward(what)
        else:
            task(t, what)

    pairing_z().wait_send()
    for part in range(M_PARTS + W_PARTS):
        for copy in [weight_z(part)] + weight_x(part):
            copy.wait_send()
    for q in range(Q):
        @pl.loop(0, PIECES)
        def _(piece):
            for l in (0, 1, 2, 3, 6, 7):
                level_copy(l, q, piece).wait_send()

        @pl.when(zb1 == q % 2)
        def _():
            @pl.loop(0, PIECES)
            def _(piece):
                for copy in (far5_copy(q, piece),) + other_copies(q, piece):
                    copy.wait_send()
            a2a_send_all(q, T - 1).wait_send()

        @pl.when(zb1 != q % 2)
        def _():
            a2a_send_all(q, T).wait_send()
    for q in range(Q):
        store(q).wait()


def body(coefficients, pairing, level_weights, middle_weights):
    bf16 = jnp.bfloat16
    dma = pltpu.SemaphoreType.DMA
    PARTS = M_PARTS + W_PARTS
    any_space = pl.BlockSpec(memory_space=pl.ANY)
    tiles = pltpu.VMEM((T, H, 2 * K), bf16)
    slots = pltpu.VMEM((B, H, 2 * K), bf16)
    return pl.pallas_call(
        kernel,
        out_shape=jax.ShapeDtypeStruct((B, C, K), bf16),
        in_specs=[any_space, pl.BlockSpec(memory_space=pltpu.SMEM), any_space, any_space, any_space],
        out_specs=any_space,
        scratch_shapes=[
            pltpu.VMEM((B, C, K), bf16),
            pltpu.VMEM((LEVELS, B, K, 2 * K), bf16),
            pltpu.VMEM((B, K, K), bf16),
            pltpu.VMEM((B, K, 2 * K), bf16),
            pltpu.VMEM((B // 2, K, 2 * K), bf16),
            pltpu.VMEM((B // 2, K, 2 * K), bf16),
            pltpu.VMEM((LEVELS, 1, B), jnp.int32),
            pltpu.SMEM((LEVELS, 1, B), jnp.int32),
            pltpu.VMEM((B, C, K), bf16),
            dma, dma((LEVELS,)), dma, dma((Q,)), dma, dma((Q,)),
            dma((LEVELS, Q, PIECES)), dma((LEVELS, Q, PIECES)), dma((Q,)), dma((Q,)),
            dma((3, Q, PIECES)), dma((2, Q, PIECES)), dma((PARTS,)), dma((PARTS,)), dma((PARTS, X - 1)), dma((PARTS, X - 1)), dma((2,)),
        ] + [tiles] * (16 * Q) + [slots] * (2 * Q),
        compiler_params=pltpu.CompilerParams(
            collective_id=0, has_side_effects=True, vmem_limit_bytes=52 * 1024 * 1024),
    )(coefficients, pairing, pairing, level_weights, middle_weights)


def solution(mesh):
    placed = (
        P("src", "rhs", None),
        P(None, "src", None),
        P(None, "src", None, None),
        P("src", None, None),
    )
    return jax.shard_map(
        body, mesh=mesh, in_specs=placed, out_specs=P("src", "rhs", None), check_vma=False
    )
```

```python
import jax
import jax.numpy as jnp
from jax import lax
from jax.experimental import pallas as pl
from jax.experimental.pallas import tpu as pltpu
from jax.sharding import PartitionSpec as P

LEVELS = 8
N = 64
B = 64
K = 64
C = 64
Q = 4
H = C // Q
T = B // 2
PIECES = 2
PT = T // PIECES
X = 4
MESH = pl.DeviceIdType.MESH
M_PARTS, W_PARTS = 1, 2
FIRST = 1
ORDER = (
    (0, (0,)), (0, (1,)), ("z", 1), (0, (2,)), (0, (3,)), ("z", 2),
    (1, (0,)), (1, (1,)), ("x", 0), (1, (2,)), (1, (3,)), ("x", 1),
    (2, (0,)), (2, (1,)), ("x", 2), (2, (2,)), (2, (3,)),
    (3, (0,)), (3, (1,)), (3, (2,)), (3, (3,)),
    (4, (0,)), (4, (1,)), (4, (2,)), (4, (3,)),
    (5, (0,)), (6, (0,)), (5, (1,)), (6, (1,)), (5, (2,)), (6, (2,)), (5, (3,)), (6, (3,)),
    (7, (0,)), (7, (1,)), (7, (2,)), (7, (3,)),
)


def kernel(coef, pairing, pairing_any, lw, mw, out,
           x_in, w, m, w_x, m_x, m_send, pair_v, pair_s, y_out,
           in_sem, w_sem, m_sem, out_sem, pair_sem, own_sem,
           lvl_send, lvl_recv, a_send, a_recv, e_send, e_recv, wz_send, wz_recv, wx_send, wx_recv, pz_sem,
           *per_chunk):
    me = lax.axis_index("src")
    rhs = lax.axis_index("rhs")
    z = me // 8
    zb1 = (z // 2) % 2

    lists = [per_chunk[i * Q:(i + 1) * Q] for i in range(len(per_chunk) // Q)]
    s0, s1, s2, s3, s4, s5, s6, s7, r0, r1, r2, r3, r5, r6, r7, other5, moved, t4 = lists
    state, far_of = (s0, s1, s2, s3, s4, s5, s6, s7), (r0, r1, r2, r3, None, r5, r6, r7)

    load_x = pltpu.make_async_copy(coef, x_in, in_sem)
    load_x.start()
    load_w = [pltpu.make_async_copy(lw.at[l], w.at[l], w_sem.at[l]) for l in range(LEVELS)]
    load_m = pltpu.make_async_copy(mw, m, m_sem)
    load_m.start()

    def flipped(s, h):
        return s + (1 << h) * (1 - 2 * ((s // (1 << h)) % 2))

    e16, e32 = flipped(me, 4), flipped(me, 5)
    e48 = flipped(e16, 5)
    far_x = [(rhs + k) % X for k in range(1, X)]
    barrier = pltpu.get_barrier_semaphore()

    @pl.loop(1, N)
    def _(k):
        pl.semaphore_signal(barrier, inc=1, device_id=((me + k) % N, rhs), device_id_type=MESH)

    for x in far_x:
        pl.semaphore_signal(barrier, inc=1, device_id=(me, x), device_id_type=MESH)
    for l in range(LEVELS):
        load_w[l].start()

    def remote(src, dst, send, recv, dev, x=None):
        return pltpu.make_async_remote_copy(
            src_ref=src, dst_ref=dst, send_sem=send, recv_sem=recv,
            device_id=(dev, rhs if x is None else x), device_id_type=MESH)

    def level_copy(l, q, piece):
        tiles = pl.ds(piece * PT, PT)
        return remote(state[l][q].at[tiles], far_of[l][q].at[tiles],
                      lvl_send.at[l, q, piece], lvl_recv.at[l, q, piece], flipped(me, l % 6))

    def a2a_copy(q, i, e):
        return remote(s4[q].at[i], moved[q].at[me], a_send.at[q], a_recv.at[q], e)

    def a2a_own(q, i):
        return pltpu.make_async_copy(s4[q].at[i], moved[q].at[me], own_sem.at[q])

    def a2a_recv_all(q):
        return remote(moved[q].at[pl.ds(0, N - 1)], moved[q].at[pl.ds(0, N - 1)], a_send.at[q], a_recv.at[q], e16)

    def a2a_send_all(q, n):
        return remote(s4[q].at[pl.ds(0, n)], s4[q].at[pl.ds(0, n)], a_send.at[q], a_recv.at[q], e16)

    def far5_copy(q, piece):
        tiles = pl.ds(piece * PT, PT)
        return remote(s5[q].at[tiles], r5[q].at[tiles], e_send.at[0, q, piece], e_recv.at[0, q, piece], e32)

    def other_copies(q, piece):
        tiles = pl.ds(piece * PT, PT)
        src = other5[q].at[tiles]
        return (remote(src, r5[q].at[tiles], e_send.at[1, q, piece], e_recv.at[0, q, piece], e48),
                remote(src, s5[q].at[tiles], e_send.at[2, q, piece], e_recv.at[1, q, piece], e16))

    def weight_part(part):
        if part < M_PARTS:
            blocks = T // X // M_PARTS
            return m_send, m_x, pl.ds(rhs * (T // X) + part * blocks, blocks)
        blocks = B // X // W_PARTS
        return lw.at[4], w_x, pl.ds(rhs * (B // X) + (part - M_PARTS) * blocks, blocks)

    def weight_z(part):
        src, dst, blocks = weight_part(part)
        return remote(src.at[blocks], dst.at[blocks], wz_send.at[part], wz_recv.at[part], e16)

    def weight_x(part):
        _, ref, blocks = weight_part(part)
        return [remote(ref.at[blocks], ref.at[blocks], wx_send.at[part, k], wx_recv.at[part, k], me, far_x[k])
                for k in range(X - 1)]

    def pairing_z():
        return remote(pairing_any, pair_v, pz_sem.at[0], pz_sem.at[1], e16)

    low_w = lax.broadcasted_iota(jnp.int32, (K, 2 * K), 1) < K
    low_t = lax.broadcasted_iota(jnp.int32, (H, 2 * K), 1) < K

    def turned(x):
        return jnp.concatenate([x[:, K:], x[:, :K]], axis=1)

    def lo(x):
        return jnp.where(low_w, x, jnp.zeros_like(x))

    def hi(x):
        return jnp.where(low_w, jnp.zeros_like(x), x)

    def first_rows(pair):
        return jnp.concatenate([lo(pair), hi(pair)], axis=1)

    def second_rows(pair):
        back = turned(pair)
        return jnp.concatenate([hi(back), lo(back)], axis=1)

    def times(x, *rows):
        weight = jnp.concatenate(rows, axis=0)
        return lax.dot_general(x, weight, (((1,), (1,)), ((), ())), preferred_element_type=jnp.float32)

    def beside(own, far):
        return jnp.concatenate([own, far], axis=1)

    def bf16(x):
        return x.astype(jnp.bfloat16)

    def gathered(ref, p, half):
        tile = ref[((p >> 5) << 4) | (p & 15)]
        return jnp.where(((p >> 4) & 1) == half, tile, turned(tile))

    def pair_level(l, qs, i, b):
        first, second = pairing[l, 0, b], pairing[l, 0, b + 16]
        tiles = []
        for q in qs:
            far = jnp.where(low_t, gathered(far_of[l][q], second, 0), gathered(far_of[l][q], first, 1))
            tiles.append(beside(state[l][q][i], far))
        new = bf16(times(jnp.concatenate(tiles, axis=0), first_rows(w[l, b]), second_rows(w[l, b + 16])))
        return [new[k * H:(k + 1) * H] for k in range(len(qs))]

    def pack(q):
        @pl.loop(0, PIECES)
        def _(piece):
            for j in range(PT):
                b = piece * 2 * PT + j
                s0[q][piece * PT + j] = beside(x_in[b, q * H:(q + 1) * H, :], x_in[b + 16, q * H:(q + 1) * H, :])

    def send_first(q):
        @pl.loop(0, PIECES)
        def _(piece):
            level_copy(0, q, piece).start()

    def wait_level(l, q):
        @pl.loop(0, PIECES)
        def _(piece):
            level_copy(l, q, piece).wait_recv()

    def store(q, piece):
        blocks, rows = pl.ds(piece * 2 * PT, 2 * PT), pl.ds(q * H, H)
        return pltpu.make_async_copy(y_out.at[blocks, rows], out.at[blocks, rows], out_sem.at[q, piece])

    def plain_level(l, qs):
        @pl.loop(0, PIECES)
        def _(piece):
            for j in range(PT):
                i, b = piece * PT + j, piece * 2 * PT + j
                for q, new in zip(qs, pair_level(l, qs, i, b)):
                    if l < LEVELS - 1:
                        state[l + 1][q][i] = new
                    else:
                        y_out[b, q * H:(q + 1) * H, :] = new[:, :K]
                        y_out[b + 16, q * H:(q + 1) * H, :] = new[:, K:]
            if l < LEVELS - 1:
                for q in qs:
                    level_copy(l + 1, q, piece).start()
            else:
                for q in qs:
                    store(q, piece).start()

    def last_source_level(qs):
        @pl.loop(0, PIECES)
        def _(step):
            piece = (step + z // 4) % PIECES
            for j in range(PT):
                i, b = piece * PT + j, piece * 2 * PT + j
                for q, new in zip(qs, pair_level(3, qs, i, b)):
                    s4[q][i] = turned(new) if q % 2 else new

            @pl.loop(0, PT)
            def _(j):
                i = piece * PT + j
                for q in qs:
                    e = piece * 2 * PT + j + 16 * (q % 2)

                    @pl.when(e != me)
                    def _():
                        a2a_copy(q, i, e).start()

                    @pl.when(e == me)
                    def _():
                        a2a_own(q, i).start()

    def middle(q):
        a2a_recv_all(q).wait_recv()
        a2a_own(q, 0).wait()

        @pl.loop(0, 2)
        def _(part):
            for j in range(B // 4):
                d = part * (B // 4) + j
                theirs = m_x[d]
                zero = jnp.zeros((K, K), jnp.bfloat16)
                for s, other in ((d, hi(theirs)), (d + B // 2, hi(turned(theirs)))):
                    t4[q][s] = bf16(times(moved[q][s], beside(m[s], zero), other))

    def level4(q):
        @pl.loop(0, PIECES)
        def _(piece):
            for j in range(PT):
                i, first = piece * PT + j, piece * 2 * PT + j
                new = []
                for b, swap in ((first, False), (first + 16, True)):
                    far = jnp.where(low_t, t4[q][pair_s[4, 0, b]], t4[q][pairing[4, 0, b]])
                    rows = first_rows(w[4, b]), second_rows(w_x[b])
                    new.append(times(beside(t4[q][b], far), *(rows[::-1] if swap else rows)))
                s5[q][i] = bf16(jnp.where(low_t, new[0], new[1]))
                other5[q][i] = turned(bf16(jnp.where(low_t, new[1], new[0])))
            for copy in (far5_copy(q, piece),) + other_copies(q, piece):
                copy.start()

    def wait_level5(q):
        @pl.loop(0, PIECES)
        def _(piece):
            far5_copy(q, piece).wait_recv()

        @pl.when(zb1 != q % 2)
        def _():
            @pl.loop(0, PIECES)
            def _(piece):
                other_copies(q, piece)[1].wait_recv()

    waited = set()

    def need(*names):
        for name in names:
            if name not in waited:
                waited.add(name)
                if name == "m of e16":
                    for part in range(M_PARTS):
                        for copy in weight_x(part):
                            copy.wait_recv()
                elif name == "w of e16":
                    for part in range(M_PARTS, M_PARTS + W_PARTS):
                        for copy in weight_x(part):
                            copy.wait_recv()
                    pairing_z().wait_recv()
                    to_smem = pltpu.make_async_copy(pair_v, pair_s, pair_sem)
                    to_smem.start()
                    to_smem.wait()
                else:
                    load_w[name].wait()

    def forward(part):
        weight_z(part).wait_recv()
        for copy in weight_x(part):
            copy.start()

    def task(t, qs):
        if t == 4:
            need("m of e16")
            for q in qs:
                @pl.when(zb1 == q % 2)
                def _():
                    middle(q)

            need("w of e16", 4)
            for q in qs:
                @pl.when(zb1 == q % 2)
                def _():
                    level4(q)
            return
        need(t)
        for q in qs:
            if t == 5:
                wait_level5(q)
            else:
                wait_level(t, q)
        if t == 3:
            last_source_level(qs)
        else:
            plain_level(t, qs)
    load_m.wait()
    for d in range(T):
        m_send[d] = beside(m[d + T], m[d])
    load_x.wait()
    pack(0)
    pl.semaphore_wait(barrier, N - 1 + X - 1)
    send_first(0)
    for part in range(FIRST):
        weight_z(part).start()
    pairing_z().start()
    for q in range(1, Q):
        pack(q)
        send_first(q)
    for t, what in ORDER:
        if t == "z":
            weight_z(what).start()
        elif t == "x":
            forward(what)
        else:
            task(t, what)

    pairing_z().wait_send()
    for part in range(M_PARTS + W_PARTS):
        for copy in [weight_z(part)] + weight_x(part):
            copy.wait_send()
    for q in range(Q):
        @pl.loop(0, PIECES)
        def _(piece):
            for l in (0, 1, 2, 3, 6, 7):
                level_copy(l, q, piece).wait_send()

        @pl.when(zb1 == q % 2)
        def _():
            @pl.loop(0, PIECES)
            def _(piece):
                for copy in (far5_copy(q, piece),) + other_copies(q, piece):
                    copy.wait_send()
            a2a_send_all(q, T - 1).wait_send()

        @pl.when(zb1 != q % 2)
        def _():
            a2a_send_all(q, T).wait_send()
    for q in range(Q):
        @pl.loop(0, PIECES)
        def _(piece):
            store(q, piece).wait()


def body(coefficients, pairing, level_weights, middle_weights):
    bf16 = jnp.bfloat16
    dma = pltpu.SemaphoreType.DMA
    PARTS = M_PARTS + W_PARTS
    any_space = pl.BlockSpec(memory_space=pl.ANY)
    tiles = pltpu.VMEM((T, H, 2 * K), bf16)
    slots = pltpu.VMEM((B, H, 2 * K), bf16)
    return pl.pallas_call(
        kernel,
        out_shape=jax.ShapeDtypeStruct((B, C, K), bf16),
        in_specs=[any_space, pl.BlockSpec(memory_space=pltpu.SMEM), any_space, any_space, any_space],
        out_specs=any_space,
        scratch_shapes=[
            pltpu.VMEM((B, C, K), bf16),
            pltpu.VMEM((LEVELS, B, K, 2 * K), bf16),
            pltpu.VMEM((B, K, K), bf16),
            pltpu.VMEM((B, K, 2 * K), bf16),
            pltpu.VMEM((B // 2, K, 2 * K), bf16),
            pltpu.VMEM((B // 2, K, 2 * K), bf16),
            pltpu.VMEM((LEVELS, 1, B), jnp.int32),
            pltpu.SMEM((LEVELS, 1, B), jnp.int32),
            pltpu.VMEM((B, C, K), bf16),
            dma, dma((LEVELS,)), dma, dma((Q, PIECES)), dma, dma((Q,)),
            dma((LEVELS, Q, PIECES)), dma((LEVELS, Q, PIECES)), dma((Q,)), dma((Q,)),
            dma((3, Q, PIECES)), dma((2, Q, PIECES)), dma((PARTS,)), dma((PARTS,)), dma((PARTS, X - 1)), dma((PARTS, X - 1)), dma((2,)),
        ] + [tiles] * (16 * Q) + [slots] * (2 * Q),
        compiler_params=pltpu.CompilerParams(
            collective_id=0, has_side_effects=True, vmem_limit_bytes=52 * 1024 * 1024),
    )(coefficients, pairing, pairing, level_weights, middle_weights)


def solution(mesh):
    placed = (
        P("src", "rhs", None),
        P(None, "src", None),
        P(None, "src", None, None),
        P("src", None, None),
    )
    return jax.shard_map(
        body, mesh=mesh, in_specs=placed, out_specs=P("src", "rhs", None), check_vma=False
    )
```
